32 devices in a mesh: dp: 2 (over x), expert: 16 (over z, y, core).
Axes of the slice: x: 2, y: 2, z: 4, core: 2. Of those that a mesh axis runs over, the one named last changes fastest.
Arguments:
- tokens: bfloat16 [512, 4096], P(('dp', 'expert')), may hold values from -6 to 6
- route_ids: int32 [512, 8], P(('dp', 'expert')), may hold values from 0 to 31, all different within a row; in each aligned block of 16 rows (0 to 15, 16 to 31, ...) at most 8 rows name the same one
- gate_weights: float32 [512, 8], P(('dp', 'expert')), may hold values from 0.05 to 0.3
- tenant_ids: int32 [512], P(('dp', 'expert')), may hold values from 0 to 3
- up_weight: bfloat16 [32, 4096, 1024], P('expert', 'dp'), may hold values from -0.09375 to 0.09375
- down_weight: bfloat16 [32, 1024, 4096], P('expert', None, 'dp'), may hold values from -0.1875 to 0.1875
- adapter_in: bfloat16 [32, 4096, 64], P('expert', 'dp'), may hold values from -0.09375 to 0.09375
- adapter_out: bfloat16 [32, 64, 1024], P('expert'), may hold values from -1.5 to 1.5
Outputs:
- mixed: bfloat16 [512, 4096], P(('dp', 'expert'))
The draws below stay inside these ranges and needn't reach their ends.
Inputs may be any that keep to these rules, and one draw needn't show every extreme that they name: `route_ids`: the 8 experts of one token differ; among the 16 tokens of one device no expert is named more than 8 times, and some expert is named 8 times.
All inputs are finite; a program needn't handle non-finite values.
Results may differ from the reference program's by a relative error of at most 0.025.
Values may be sent and summed in bfloat16 or wider, within the bound.
A program may use at most 64 MiB of HBM per device.

```python
import math
import jax
import jax.numpy as jnp
import numpy as np
from jax import lax

D = 4096
F = 1024
EXPERTS = 32
TOP = 8
TEN = 4
RANK = 16
TOK_DEV = 16
TOKENS = 512
CAPE = 8
N_DP = 2


def plant(drawn, own_key, low, top_value):
    longest = drawn.shape.index(max(drawn.shape))
    spots = []
    for shift in (0, 1):
        where = [jax.random.randint(jax.random.fold_in(own_key, axis), (), 0, length) for axis, length in enumerate(drawn.shape)]
        where[longest] = (where[longest] + shift) % drawn.shape[longest]
        spots.append(tuple(where))
    return drawn.at[spots[0]].set(low).at[spots[1]].set(top_value)


def levels(rng, extent, split, smallest, high):
    gain = 1.0
    for axis_at, shards_of in split:
        heights = jax.random.uniform(jax.random.fold_in(jax.random.fold_in(rng, 6), axis_at), (shards_of,), jnp.float32, smallest / len(split), high / len(split))
        gain = gain * jnp.repeat(jnp.exp(heights), extent[axis_at] // shards_of).reshape((-1,) + (1,) * (len(extent) - 1 - axis_at))
    return gain


def deal_out(stream_key, own, number, rows, count, top, reach, lean):
    order = jax.random.permutation(stream_key, count)
    heavy_load, ordinary = portions_of(count, rows * top, reach, lean, True), portions_of(count, rows * top, reach, lean, False)
    places = jnp.arange(count)

    def named(sizes, rotation):
        used = int((sizes > 0).sum())
        fixed = max(1, used // 4)
        shifted = fixed + (places - fixed + rotation * (used - fixed)) % max(1, count - fixed)
        return jnp.zeros((count,), jnp.int32).at[order[jnp.where(places < fixed, places, shifted)]].set(jnp.asarray(sizes, jnp.int32))

    sizes = jnp.where(number % 4 == 0, named(heavy_load, number // 4), named(ordinary, number - number // 4 - 1))
    mixed = jax.random.permutation(jax.random.fold_in(own, 3), count)
    giver, receiver = mixed[0:count // 2 * 2:2], mixed[1:count // 2 * 2:2]
    slack = jnp.minimum(sizes[giver] - 1, reach - sizes[receiver]) // 2
    slack = jnp.where((giver == order[0]) | (receiver == order[0]) | (sizes[receiver] == 0), 0, jnp.maximum(slack, 0))
    shifted = jax.random.randint(jax.random.fold_in(own, 4), (count // 2,), 0, 1 << 20) % (slack + 1)
    sizes = sizes.at[giver].add(-shifted).at[receiver].add(shifted)
    members = jnp.searchsorted(jnp.cumsum(sizes), jnp.arange(rows * top), side="right").astype(jnp.int32)
    grid = members.reshape(top, rows).T
    grid = grid[jax.random.permutation(jax.random.fold_in(own, 1), rows)]
    rotation = jax.random.randint(jax.random.fold_in(own, 2), (rows, 1), 0, top)
    return jnp.take_along_axis(grid, (jnp.arange(top)[None, :] + rotation) % top, axis=1)


def portions_of(amount, total, bound, slope, full):
    weights = [(1 << 20) // math.isqrt(rank ** slope) + 1 for rank in range(1, amount + 1)]
    largest = bound if full else min(bound, max(-(-total // amount), total * weights[0] // sum(weights)))
    least = 1 if total - largest >= amount - 1 else 0
    counts, spare = [largest] + [least] * (amount - 1), total - largest - least * (amount - 1)
    while spare > 0:
        movable = [i for i in range(1, amount) if counts[i] < largest] or [i for i in range(1, amount) if counts[i] < bound]
        mass, budget = sum([weights[i] for i in movable]), spare
        for i in movable:
            more = min(bound - counts[i], max(1, budget * weights[i] // mass), spare)
            counts[i] = counts[i] + more
            spare = spare - more
    return np.array(counts)


def normal_values(key, dims, width, reach, pieces=(), kind=jnp.bfloat16):
    result = width * jax.random.normal(key, dims, jnp.float32)
    if pieces:
        result = result * levels(key, dims, pieces, -0.22, 0.18)
    return jnp.clip(result, -reach, reach).astype(kind)


def setup_inputs(seed: int = 0) -> dict:
    key_list = jax.random.split(jax.random.key(seed), 9)
    tokens = normal_values(key_list[0], (TOKENS, D), 1.0, 6.0, ((0, 32),))
    route_ids_keys = jax.random.split(jax.random.fold_in(key_list[1], 1), TOKENS // TOK_DEV)
    route_ids_turns = jax.random.permutation(jax.random.fold_in(key_list[1], 3), TOKENS // TOK_DEV)
    route_ids = jax.vmap(lambda own, number: deal_out(jax.random.fold_in(key_list[1], 2), own, number, TOK_DEV, EXPERTS, TOP, CAPE, 2))(route_ids_keys, route_ids_turns).reshape((TOKENS, TOP))
    gate_weights = jnp.clip(0.05 + 0.25 * jax.random.uniform(key_list[2], (TOKENS, TOP), jnp.float32) ** levels(key_list[2], (TOKENS, TOP), ((0, 32),), -0.2, 0.2), 0.05, 0.3)
    tenant_ids = plant(jax.random.randint(key_list[3], (TOKENS,), 0, TEN), jax.random.fold_in(key_list[3], 1), 0, TEN - 1).astype(jnp.int32)
    up_weight = normal_values(key_list[4], (EXPERTS, D, F), D ** -0.5, 0.09375, ((0, 16), (1, 2)))
    down_weight = normal_values(key_list[5], (EXPERTS, F, D), F ** -0.5, 0.1875, ((0, 16), (2, 2)))
    adapter_in = normal_values(key_list[6], (EXPERTS, D, TEN * RANK), D ** -0.5, 0.09375, ((0, 16), (1, 2)))
    adapter_out = normal_values(key_list[7], (EXPERTS, TEN * RANK, F), RANK ** -0.5, 1.5, ((0, 16),))
    return {"tokens": tokens, "route_ids": route_ids, "gate_weights": gate_weights, "tenant_ids": tenant_ids, "up_weight": up_weight, "down_weight": down_weight, "adapter_in": adapter_in, "adapter_out": adapter_out}


def reference(tokens, route_ids, gate_weights, tenant_ids, up_weight, down_weight, adapter_in, adapter_out):
    total = tokens.shape[0]
    devices = total // TOK_DEV
    per_dev = TOK_DEV * TOP
    flat_routes = route_ids.reshape(devices, per_dev)
    same = flat_routes[:, :, None] == flat_routes[:, None, :]
    order = jnp.arange(per_dev, dtype=jnp.int32)
    earlier = order[None, :] < order[:, None]
    rank = jnp.sum((same & earlier[None]).astype(jnp.int32), axis=2).astype(jnp.int32)
    device_ids = jnp.arange(devices, dtype=jnp.int32)[:, None]
    position = (device_ids * CAPE + rank).reshape(-1).astype(jnp.int32)
    expert_of = flat_routes.reshape(-1).astype(jnp.int32)
    token_of = jnp.repeat(jnp.arange(total, dtype=jnp.int32), TOP)
    depth = devices * CAPE
    slot_index = (expert_of * depth + position).astype(jnp.int32)
    table = jnp.full((EXPERTS * depth,), -1, jnp.int32).at[slot_index].set(token_of)
    piece = D // N_DP
    columns = jnp.arange(TEN * RANK, dtype=jnp.int32) // RANK

    def one_expert(args):
        rows, w_up, w_down, a_in, adapter_expand_output = args
        live = rows >= 0
        safe = jnp.maximum(rows, 0).astype(jnp.int32)
        gathered = jnp.where(live[:, None], tokens[safe], jnp.zeros((), tokens.dtype))
        blocks = gathered.reshape(depth, N_DP, piece).astype(jnp.float32)
        up_parts = jnp.einsum('spd,pdf->spf', blocks, w_up.reshape(N_DP, piece, F).astype(jnp.float32))
        up_projected = jnp.sum(up_parts.astype(jnp.bfloat16).astype(jnp.float32), axis=1)
        shrink_parts = jnp.einsum('spd,pdr->spr', blocks, a_in.reshape(N_DP, piece, TEN * RANK).astype(jnp.float32))
        shrink = jnp.sum(shrink_parts.astype(jnp.bfloat16).astype(jnp.float32), axis=1)
        tenant = jnp.where(live, tenant_ids[safe], -1)
        keep = columns[None, :] == tenant[:, None]
        masked_values = jnp.where(keep, shrink, jnp.zeros((), jnp.float32))
        low_rank_adapter = jnp.dot(masked_values, adapter_expand_output.astype(jnp.float32), precision=lax.Precision.HIGHEST)
        hidden_activations = jax.nn.silu(up_projected + low_rank_adapter).astype(jnp.bfloat16)
        return jnp.dot(hidden_activations, w_down, preferred_element_type=jnp.float32).astype(jnp.bfloat16)

    outputs = lax.map(one_expert, (table.reshape(EXPERTS, depth), up_weight, down_weight, adapter_in, adapter_out))
    results = outputs.reshape(EXPERTS * depth, D)
    slots_grid = slot_index.reshape(total, TOP)

    def add_choice(acc, k):
        picked = results[slots_grid[:, k]].astype(jnp.float32)
        return acc + picked * gate_weights[:, k][:, None], None

    mixed, _ = lax.scan(add_choice, jnp.zeros((total, D), jnp.float32), jnp.arange(TOP, dtype=jnp.int32))
    return mixed.astype(jnp.bfloat16)
```

```python
import functools

import jax
import jax.numpy as jnp
from jax import lax
from jax.experimental import pallas as pl
from jax.experimental.pallas import tpu as pltpu
from jax.sharding import PartitionSpec as P

RANK = 16
MESH = pl.DeviceIdType.MESH
BF = jnp.bfloat16
F32 = jnp.float32
LANES = 128
NZ = 4


def expert_kernel(
    dims,
    xe,
    w_up_hbm,
    w_down_hbm,
    a_in_hbm,
    a_out_hbm,
    out,
    w_up,
    w_down,
    a_in,
    a_out,
    grid,
    packed,
    pick,
    part,
    peer,
    rows_out,
    y_part,
    core_in,
    y_send,
    y_in,
    z_send,
    z_in,
    x_send,
    x_in,
    load_sem,
    tx_s,
    tx_r,
    ty_s,
    ty_r,
    tz_s,
    tz_r,
    tc_s,
    tc_r,
    tw_s,
    tw_r,
    v_s,
    v_r,
    c_s,
    c_r,
    y_s,
    y_r,
    z_s,
    z_r,
    x_s,
    x_r,
):
    tok, cap, piece, units, cols = dims
    unit = 2 * tok
    chunk = 2 * NZ * unit
    rows = (chunk // tok) * cap
    x = lax.axis_index("dp")
    e = lax.axis_index("expert")
    z = e // 4
    y = (e // 2) % 2
    c = e % 2
    x_dev = (1 - x, e)
    y_dev = (x, z * 4 + (1 - y) * 2 + c)
    c_dev = (x, z * 4 + y * 2 + (1 - c))

    def z_dev(d):
        return (x, lax.rem(z + d, NZ) * 4 + y * 2 + c)

    def place(core, zz):
        return pl.ds(pl.multiple_of((core * NZ + zz) * unit, unit), unit)

    def remote(src, dst, ss, rs, dev):
        return pltpu.make_async_remote_copy(
            src_ref=src, dst_ref=dst, send_sem=ss, recv_sem=rs, device_id=dev, device_id_type=MESH
        )

    loads = [
        pltpu.make_async_copy(w_up_hbm, w_up, load_sem.at[0]),
        pltpu.make_async_copy(a_in_hbm, a_in, load_sem.at[1]),
        pltpu.make_async_copy(a_out_hbm, a_out, load_sem.at[2]),
        pltpu.make_async_copy(w_down_hbm, w_down, load_sem.at[3]),
    ]
    for copy in loads:
        copy.start()

    barrier = pltpu.get_barrier_semaphore()
    for dev in [x_dev, y_dev, c_dev] + [z_dev(d) for d in range(1, NZ)]:
        pl.semaphore_signal(barrier, inc=1, device_id=dev, device_id_type=MESH)
    pl.semaphore_wait(barrier, 3 + NZ - 1)

    def half(dp):
        return pl.ds(pl.multiple_of((c * NZ + z) * unit + dp * tok, tok), tok)

    sends = []
    cp = remote(xe.at[1 - x], grid.at[1, half(x)], tx_s, tx_r, x_dev)
    cp.start()
    sends.append(cp)
    grid[1, half(x), :] = xe[x]
    remote(xe.at[1 - x], grid.at[1, half(1 - x)], tx_s, tx_r, x_dev).wait_recv()

    own = place(c, z)
    cp = remote(grid.at[1, own], grid.at[0, own], ty_s.at[0], ty_r.at[0], y_dev)
    cp.start()
    sends.append(cp)
    cp1 = remote(grid.at[1, own], grid.at[1, own], tw_s.at[0], tw_r.at[0], c_dev)
    cp1.start()
    sends.append(cp1)
    cp.wait_recv()
    for d in (2, 1, 3):
        cp = remote(grid.at[0, own], grid.at[0, own], tz_s.at[d], tz_r.at[d], z_dev(d))
        cp.start()
        sends.append(cp)
    cp = remote(grid.at[0, own], grid.at[0, own], tc_s.at[0], tc_r.at[0], c_dev)
    cp.start()
    sends.append(cp)
    for d in (1, 3, 2):
        there = place(c, lax.rem(z + NZ - d, NZ))
        remote(grid.at[0, there], grid.at[0, there], tz_s.at[d], tz_r.at[d], z_dev(d)).wait_recv()
        cp = remote(grid.at[0, there], grid.at[0, there], tc_s.at[d], tc_r.at[d], c_dev)
        cp.start()
        sends.append(cp)
        cp = remote(grid.at[0, there], grid.at[1, there], ty_s.at[d], ty_r.at[d], y_dev)
        cp.start()
        sends.append(cp)

    def from_core(k, ss, rs):
        for d in (0, 1, 3, 2):
            there = place(1 - c, lax.rem(z + NZ - d, NZ))
            remote(grid.at[k, there], grid.at[k, there], ss.at[d], rs.at[d], c_dev).wait_recv()

    def compact(k):
        meta = grid[k, :, piece:]
        eye = (
            lax.broadcasted_iota(jnp.int32, (LANES, LANES), 0)
            == lax.broadcasted_iota(jnp.int32, (LANES, LANES), 1)
        ).astype(F32).astype(BF)
        flat = lax.dot_general(
            eye, meta, (((1,), (1,)), ((), ())), preferred_element_type=F32
        )
        t0 = lax.broadcasted_iota(jnp.int32, (chunk, chunk), 0)
        t1 = lax.broadcasted_iota(jnp.int32, (chunk, chunk), 1)
        before = jnp.where((t0 // tok == t1 // tok) & (t0 < t1), 1.0, 0.0).astype(BF)
        r0 = lax.broadcasted_iota(jnp.int32, (rows, chunk), 0)
        r1 = lax.broadcasted_iota(jnp.int32, (rows, chunk), 1)
        same = r0 // cap == r1 // tok
        slot = (r0 % cap).astype(F32)
        for j in range(2):
            expert = (2 * e + j).astype(F32)
            named = jnp.sum(jnp.where(flat[0:8] == expert, 1.0, 0.0), axis=0, keepdims=True)
            named = jnp.broadcast_to(named, (16, chunk))
            rank = jnp.dot(named.astype(BF), before, preferred_element_type=F32)
            hit = same & (slot == rank[0:1]) & (named[0:1] > 0.5)
            pick[k, j * rows : (j + 1) * rows, :] = jnp.where(hit, 1.0, 0.0).astype(BF)
        width = piece + LANES
        step = LANES

        def body(n, carry):
            at = pl.ds(pl.multiple_of(n * step, step), step)
            packed[k, :, at] = jnp.dot(
                pick[k], grid[k, :, at], preferred_element_type=F32
            ).astype(BF)
            return carry

        lax.fori_loop(0, width // step, body, 0)

    def up(k, j):
        here = pl.ds(j * rows, rows)
        low = jnp.dot(packed[k, here, 0:piece], a_in[j], preferred_element_type=F32)
        tenant = packed[k, here, piece + 24 : piece + 25].astype(F32)
        owner = (lax.broadcasted_iota(jnp.int32, (rows, cols), 1) // RANK).astype(F32)
        low = jnp.where(owner == tenant, low, 0.0).astype(BF)
        step = 256

        def body(n, carry):
            at = pl.ds(pl.multiple_of(n * step, step), step)
            value = jnp.dot(
                packed[k, here, 0:piece], w_up[j, :, at], preferred_element_type=F32
            )
            value = value + jnp.dot(low, a_out[j, :, at], preferred_element_type=F32)
            part[k, j, :, at] = value.astype(BF)
            return carry

        lax.fori_loop(0, units // step, body, 0)
        cp = remote(part.at[k, j], peer.at[k, j], v_s.at[k, j], v_r.at[k, j], x_dev)
        cp.start()
        return cp

    def down(k, j, cp):
        cp.wait_recv()
        here = pl.ds(j * rows, rows)
        meta = packed[k, here, piece:].astype(F32)
        expert = (2 * e + j).astype(F32)
        gates = jnp.where(meta[:, 0:8] == expert, meta[:, 8:16] + meta[:, 16:24], 0.0)
        gate = jnp.sum(gates, axis=1, keepdims=True)
        value = part[k, j].astype(F32) + peer[k, j].astype(F32)
        hidden = (value / (1.0 + jnp.exp(-value))).astype(BF)
        step = 256

        def body(n, carry):
            at = pl.ds(pl.multiple_of(n * step, step), step)
            value = jnp.dot(hidden, w_down[j, :, at], preferred_element_type=F32)
            rows_out[here, at] = (value * gate).astype(BF)
            return carry

        lax.fori_loop(0, piece // step, body, 0)

    def spread(k):
        size = 2 * rows
        eye = jnp.where(
            lax.broadcasted_iota(jnp.int32, (chunk, chunk), 0)
            == lax.broadcasted_iota(jnp.int32, (chunk, chunk), 1),
            1.0,
            0.0,
        ).astype(BF)
        back = lax.dot_general(
            eye, pick[k], (((1,), (1,)), ((), ())), preferred_element_type=F32
        ).astype(BF)
        step = 256

        def body(n, carry):
            at = pl.ds(pl.multiple_of(n * step, step), step)
            y_part[k, :, at] = jnp.dot(
                back, rows_out[:, at], preferred_element_type=F32
            ).astype(BF)
            return carry

        lax.fori_loop(0, piece // step, body, 0)
        line = NZ * unit
        theirs = pl.ds(pl.multiple_of((1 - c) * line, line), line)
        cp = remote(y_part.at[k, theirs], core_in.at[k], c_s.at[k], c_r.at[k], c_dev)
        cp.start()
        return cp

    from_core(0, tc_s, tc_r)
    compact(0)
    loads[0].wait()
    loads[1].wait()
    loads[2].wait()
    v00 = up(0, 0)
    for d in (1, 3, 2):
        there = place(c, lax.rem(z + NZ - d, NZ))
        remote(grid.at[0, there], grid.at[1, there], ty_s.at[d], ty_r.at[d], y_dev).wait_recv()
        cp = remote(grid.at[1, there], grid.at[1, there], tw_s.at[d], tw_r.at[d], c_dev)
        cp.start()
        sends.append(cp)
    v01 = up(0, 1)
    from_core(1, tw_s, tw_r)
    compact(1)
    v10 = up(1, 0)
    v11 = up(1, 1)
    loads[3].wait()
    line = NZ * unit
    mine = pl.ds(pl.multiple_of(c * line, line), line)

    down(0, 0, v00)
    down(0, 1, v01)
    cc = spread(0)
    cc.wait_recv()
    y_send[...] = (y_part[0, mine].astype(F32) + core_in[0].astype(F32)).astype(BF)
    cy = remote(y_send, y_in, y_s, y_r, y_dev)
    cy.start()
    down(1, 0, v10)
    down(1, 1, v11)
    cd = spread(1)
    cy.wait_recv()
    cd.wait_recv()
    z_send[...] = (
        y_part[1, mine].astype(F32) + core_in[1].astype(F32) + y_in[...].astype(F32)
    ).astype(BF)

    def spot(zz):
        return pl.ds(pl.multiple_of(zz * unit, unit), unit)

    zs = []
    for d in (2, 1, 3):
        cp = remote(
            z_send.at[spot(lax.rem(z + d, NZ))], z_in.at[d - 1], z_s.at[d], z_r.at[d], z_dev(d)
        )
        cp.start()
        zs.append(cp)
    for cp in zs:
        cp.wait_recv()
    total = z_send[spot(z)].astype(F32)
    for d in range(1, NZ):
        total = total + z_in[d - 1].astype(F32)
    x_send[...] = total.astype(BF).reshape(2, tok, piece)
    cx = remote(x_send.at[1 - x], x_in, x_s, x_r, x_dev)
    cx.start()
    keep = x_send[x]
    cx.wait_recv()
    other = x_in[...]
    first = x == 0
    out[:, 0:piece] = jnp.where(first, keep, other)
    out[:, piece:] = jnp.where(first, other, keep)
    for cp in sends + [v00, v01, v10, v11, cc, cd, cy, cx] + zs:
        cp.wait_send()


def fused(
    tokens, route_ids, gate_weights, tenant_ids, up_weight, down_weight, adapter_in, adapter_out
):
    tok = tokens.shape[0]
    piece = up_weight.shape[1]
    units = up_weight.shape[2]
    cols = adapter_in.shape[2]
    experts_all = up_weight.shape[0] * lax.axis_size("expert")
    cap = max(2, 2 * tok * route_ids.shape[1] // experts_all)
    high = lax.reduce_precision(gate_weights, 8, 7)
    meta = jnp.concatenate(
        [
            route_ids.astype(F32),
            high,
            gate_weights - high,
            tenant_ids.astype(F32)[:, None],
            jnp.zeros((tok, LANES - 25), F32),
        ],
        axis=1,
    ).astype(BF)
    xe = jnp.stack(
        [
            jnp.concatenate([tokens[:, :piece], meta], axis=1),
            jnp.concatenate([tokens[:, piece:], meta], axis=1),
        ]
    )
    unit = 2 * tok
    chunk = 2 * NZ * unit
    rows = (chunk // tok) * cap
    line = NZ * unit
    dma = pltpu.SemaphoreType.DMA
    vm = lambda *shape: pltpu.VMEM(shape, BF)
    any_spec = pl.BlockSpec(memory_space=pl.ANY)
    vmem_spec = pl.BlockSpec(memory_space=pltpu.VMEM)
    return pl.pallas_call(
        functools.partial(expert_kernel, (tok, cap, piece, units, cols)),
        out_shape=jax.ShapeDtypeStruct(tokens.shape, BF),
        in_specs=[vmem_spec] + [any_spec] * 4,
        out_specs=vmem_spec,
        scratch_shapes=[
            vm(*up_weight.shape),
            vm(*down_weight.shape),
            vm(*adapter_in.shape),
            vm(*adapter_out.shape),
            vm(2, chunk, piece + LANES),
            vm(2, 2 * rows, piece + LANES),
            vm(2, 2 * rows, chunk),
            vm(2, 2, rows, units),
            vm(2, 2, rows, units),
            vm(2 * rows, piece),
            vm(2, chunk, piece),
            vm(2, line, piece),
            vm(line, piece),
            vm(line, piece),
            vm(line, piece),
            vm(NZ - 1, unit, piece),
            vm(2, tok, piece),
            vm(tok, piece),
            dma((4,)),
            dma,
            dma,
            dma((NZ,)),
            dma((NZ,)),
            dma((NZ,)),
            dma((NZ,)),
            dma((NZ,)),
            dma((NZ,)),
            dma((NZ,)),
            dma((NZ,)),
            dma((2, 2)),
            dma((2, 2)),
            dma((2,)),
            dma((2,)),
            dma,
            dma,
            dma((NZ,)),
            dma((NZ,)),
            dma,
            dma,
        ],
        compiler_params=pltpu.CompilerParams(
            collective_id=0, has_side_effects=True, vmem_limit_bytes=48 * 1024 * 1024
        ),
    )(xe, up_weight, down_weight, adapter_in, adapter_out)


def per_device(
    tokens, route_ids, gate_weights, tenant_ids, up_weight, down_weight, adapter_in, adapter_out
):
    n_dp = lax.axis_size("dp")
    n_col = lax.axis_size("expert")
    tok_count = tokens.shape[0]
    chosen = route_ids.shape[1]
    features = tokens.shape[1]
    exp_local = up_weight.shape[0]
    piece = up_weight.shape[1]
    units = up_weight.shape[2]
    adapter_cols = adapter_in.shape[2]
    experts_all = exp_local * n_col
    capacity = max(2, 2 * tok_count * chosen // experts_all)
    send_rows = experts_all * capacity
    flat_routes = route_ids.reshape(-1)
    order = jnp.arange(flat_routes.shape[0], dtype=jnp.int32)
    same = flat_routes[:, None] == flat_routes[None, :]
    earlier = order[None, :] < order[:, None]
    rank = jnp.sum((same & earlier).astype(jnp.int32), axis=1)
    target = flat_routes * capacity + rank
    outgoing = (
        jnp.zeros((send_rows, features), jnp.bfloat16)
        .at[target]
        .set(jnp.repeat(tokens, chosen, axis=0))
    )
    tag_line = (
        jnp.full((send_rows,), -1.0, jnp.float32)
        .at[target]
        .set(jnp.repeat(tenant_ids, chosen).astype(jnp.float32))
    )
    tag_grid = jnp.broadcast_to(tag_line[:, None], (send_rows, n_dp)).astype(jnp.bfloat16)
    sending = outgoing.reshape(n_col, exp_local, capacity, n_dp, piece)
    tag_send = tag_grid.reshape(n_col, exp_local, capacity, n_dp, 1)
    arrived, arrived_tags = (
        lax.all_to_all(
            lax.all_to_all(sending, "dp", split_axis=3, concat_axis=2, tiled=True),
            "expert",
            split_axis=0,
            concat_axis=2,
            tiled=True,
        ),
        lax.all_to_all(
            lax.all_to_all(tag_send, "dp", split_axis=3, concat_axis=2, tiled=True),
            "expert",
            split_axis=0,
            concat_axis=2,
            tiled=True,
        ),
    )
    rows_all = arrived.shape[2]
    grid = arrived.reshape(exp_local, rows_all, piece)
    tags = arrived_tags.reshape(exp_local, rows_all).astype(jnp.float32)
    up_part = jnp.einsum("erd,edf->erf", grid, up_weight, preferred_element_type=jnp.float32)
    shrink_part = jnp.einsum("erd,edl->erl", grid, adapter_in, preferred_element_type=jnp.float32)
    owner = (jnp.arange(adapter_cols, dtype=jnp.int32) // RANK).astype(jnp.float32)
    shrink = lax.psum(shrink_part.astype(jnp.bfloat16), "dp").astype(jnp.float32)
    keep = owner[None, None, :] == tags[..., None]
    masked_values = jnp.where(keep, shrink, jnp.zeros((), jnp.float32))
    up_portion = lax.psum_scatter(
        up_part.astype(jnp.bfloat16), "dp", scatter_dimension=2, tiled=True
    ).astype(jnp.float32)
    share = units // n_dp
    mapping_portion = lax.dynamic_slice_in_dim(
        adapter_out, lax.axis_index("dp") * share, share, 2
    ).astype(jnp.float32)
    low_rank_adapter = jnp.einsum(
        "erl,elf->erf", masked_values, mapping_portion, precision=lax.Precision.HIGHEST
    )
    hidden_portion = jax.nn.silu(up_portion + low_rank_adapter).astype(jnp.bfloat16)
    hidden_activations = lax.all_gather(hidden_portion, "dp", axis=2, tiled=True)
    expert_out = jnp.einsum(
        "erf,efd->erd", hidden_activations, down_weight, preferred_element_type=jnp.float32
    ).astype(jnp.bfloat16)
    going_back = expert_out.reshape(1, exp_local, rows_all, 1, piece)
    returned = lax.all_to_all(
        lax.all_to_all(going_back, "expert", split_axis=2, concat_axis=0, tiled=True),
        "dp",
        split_axis=2,
        concat_axis=3,
        tiled=True,
    )
    results = returned.reshape(send_rows, features)
    picked = results[target].astype(jnp.float32).reshape(tok_count, chosen, features)
    mixed = jnp.sum(picked * gate_weights[:, :, None], axis=1)
    return mixed.astype(jnp.bfloat16)


def solution(mesh):
    placed = (
        P(("dp", "expert"), None),
        P(("dp", "expert"), None),
        P(("dp", "expert"), None),
        P(("dp", "expert")),
        P("expert", "dp", None),
        P("expert", None, "dp"),
        P("expert", "dp", None),
        P("expert", None, None),
    )
    small = mesh.shape["dp"] == 2 and mesh.shape["expert"] == 4 * NZ
    return jax.shard_map(
        fused if small else per_device, mesh=mesh, in_specs=placed, out_specs=P(("dp", "expert"), None), check_vma=False
    )
```

```python
import functools

import jax
import jax.numpy as jnp
from jax import lax
from jax.experimental import pallas as pl
from jax.experimental.pallas import tpu as pltpu
from jax.sharding import PartitionSpec as P

RANK = 16
MESH = pl.DeviceIdType.MESH
BF = jnp.bfloat16
F32 = jnp.float32
LANES = 128
NZ = 4


def equal_iota(shape):
    same = lax.broadcasted_iota(jnp.int32, shape, 0) == lax.broadcasted_iota(jnp.int32, shape, 1)
    return jnp.where(same, 1.0, 0.0)


def expert_kernel(
    dims,
    tokens,
    routes_t,
    gates_t,
    tenants_t,
    w_up_hbm,
    w_down_hbm,
    a_in_hbm,
    a_out_hbm,
    out,
    w_up,
    w_down,
    a_in,
    a_out,
    first_out,
    grid,
    packed,
    pick,
    part,
    peer,
    rows_out,
    y_part,
    core_in,
    y_send,
    y_in,
    z_send,
    z_in,
    x_send,
    x_in,
    load_sem,
    tx_s,
    tx_r,
    ty_s,
    ty_r,
    tz_s,
    tz_r,
    tc_s,
    tc_r,
    v_s,
    v_r,
    c_s,
    c_r,
    y_s,
    y_r,
    z_s,
    z_r,
    x_s,
    x_r,
):
    tok, cap, piece, units, cols = dims
    unit = 2 * tok
    chunk = 4 * unit
    rows = (chunk // tok) * cap
    x = lax.axis_index("dp")
    e = lax.axis_index("expert")
    z = e // 4
    y = (e // 2) % 2
    c = e % 2
    x_dev = (1 - x, e)
    y_dev = (x, z * 4 + (1 - y) * 2 + c)
    c_dev = (x, z * 4 + y * 2 + (1 - c))
    z_of = {1: z + 1 - 2 * (z % 2), 2: (z + 2) % 4, 3: 3 - z}
    z_dev = {q: (x, z_of[q] * 4 + y * 2 + c) for q in z_of}

    def place(core, row):
        return pl.ds(pl.multiple_of((core * 2 + row) * unit, unit), unit)

    def remote(src, dst, ss, rs, dev):
        return pltpu.make_async_remote_copy(
            src_ref=src, dst_ref=dst, send_sem=ss, recv_sem=rs, device_id=dev, device_id_type=MESH
        )

    loads = [
        pltpu.make_async_copy(w_up_hbm, w_up, load_sem.at[0]),
        pltpu.make_async_copy(a_in_hbm, a_in, load_sem.at[1]),
        pltpu.make_async_copy(a_out_hbm, a_out, load_sem.at[2]),
        pltpu.make_async_copy(w_down_hbm, w_down, load_sem.at[3]),
    ]
    for copy in loads:
        copy.start()

    barrier = pltpu.get_barrier_semaphore()
    for dev in [x_dev, y_dev, c_dev] + [z_dev[q] for q in z_of]:
        pl.semaphore_signal(barrier, inc=1, device_id=dev, device_id_type=MESH)

    gates = gates_t[...]
    high = gates.astype(BF).astype(F32)
    stacked = jnp.concatenate(
        [
            routes_t[...].astype(F32),
            high,
            gates - high,
            jnp.broadcast_to(tenants_t[...].astype(F32), (8, tok)),
        ],
        axis=0,
    )
    meta = lax.dot_general(
        stacked, equal_iota((32, LANES)), (((0,), (0,)), ((), ())), preferred_element_type=F32
    ).astype(BF)

    def half(dp):
        return pl.ds(pl.multiple_of((c * 2 + y) * unit + dp * tok, tok), tok)

    first_out[:, 0:piece] = tokens[:, pl.ds(pl.multiple_of((1 - x) * piece, piece), piece)]
    first_out[:, piece:] = meta
    grid[0, half(x), 0:piece] = tokens[:, pl.ds(pl.multiple_of(x * piece, piece), piece)]
    grid[0, half(x), piece:] = meta
    pl.semaphore_wait(barrier, 3 + NZ - 1)

    sends = []

    def go(*args):
        cp = remote(*args)
        cp.start()
        sends.append(cp)
        return cp

    go(first_out, grid.at[0, half(x)], tx_s, tx_r, x_dev)
    remote(first_out, grid.at[0, half(1 - x)], tx_s, tx_r, x_dev).wait_recv()

    own = place(c, y)
    over = place(c, 1 - y)

    def send_y(q):
        go(grid.at[q, own], grid.at[q, own], ty_s.at[q], ty_r.at[q], y_dev)

    def wait_y(q):
        remote(grid.at[q, over], grid.at[q, over], ty_s.at[q], ty_r.at[q], y_dev).wait_recv()

    def send_z(q):
        go(grid.at[0, own], grid.at[q, own], tz_s.at[q], tz_r.at[q], z_dev[q])

    def wait_z(q):
        remote(grid.at[q, own], grid.at[q, own], tz_s.at[q], tz_r.at[q], z_dev[q]).wait_recv()

    def send_c(q, which):
        spot = own if which == 0 else over
        go(grid.at[q, spot], grid.at[q, spot], tc_s.at[q, which], tc_r.at[q, which], c_dev)

    def wait_c(q):
        for which, row in ((0, y), (1, 1 - y)):
            spot = place(1 - c, row)
            remote(
                grid.at[q, spot], grid.at[q, spot], tc_s.at[q, which], tc_r.at[q, which], c_dev
            ).wait_recv()

    def arrive_z(q):
        wait_z(q)
        send_y(q)
        send_c(q, 0)

    def arrive_y(q):
        wait_y(q)
        send_c(q, 1)

    def compact(q):
        wait_c(q)
        flat = lax.dot_general(
            equal_iota((LANES, LANES)).astype(BF),
            grid[q, :, piece:],
            (((1,), (1,)), ((), ())),
            preferred_element_type=F32,
        )
        t0 = lax.broadcasted_iota(jnp.int32, (chunk, chunk), 0)
        t1 = lax.broadcasted_iota(jnp.int32, (chunk, chunk), 1)
        before = jnp.where((t0 // tok == t1 // tok) & (t0 < t1), 1.0, 0.0).astype(BF)
        r0 = lax.broadcasted_iota(jnp.int32, (rows, chunk), 0)
        r1 = lax.broadcasted_iota(jnp.int32, (rows, chunk), 1)
        same = r0 // cap == r1 // tok
        slot = (r0 % cap).astype(F32)
        for j in range(2):
            expert = (2 * e + j).astype(F32)
            named = jnp.sum(jnp.where(flat[0:8] == expert, 1.0, 0.0), axis=0, keepdims=True)
            named = jnp.broadcast_to(named, (16, chunk))
            rank = jnp.dot(named.astype(BF), before, preferred_element_type=F32)
            hit = same & (slot == rank[0:1]) & (named[0:1] > 0.5)
            pick[q, j * rows : (j + 1) * rows, :] = jnp.where(hit, 1.0, 0.0).astype(BF)
        packed[q, :, piece:] = jnp.dot(
            pick[q], grid[q, :, piece:], preferred_element_type=F32
        ).astype(BF)
        step = 512

        def body(n, carry):
            at = pl.ds(pl.multiple_of(n * step, step), step)
            packed[q, :, at] = jnp.dot(
                pick[q], grid[q, :, at], preferred_element_type=F32
            ).astype(BF)
            return carry

        lax.fori_loop(0, piece // step, body, 0)

    values = {}

    def up(q):
        compact(q)
        if q == 0:
            loads[0].wait()
            loads[1].wait()
            loads[2].wait()
        for j in range(2):
            here = pl.ds(j * rows, rows)
            low = lax.dot_general(
                packed[q, here, 0:piece],
                a_in[j],
                (((1,), (1,)), ((), ())),
                preferred_element_type=F32,
            )
            tenant = packed[q, here, piece + 24 : piece + 25].astype(F32)
            owner = (lax.broadcasted_iota(jnp.int32, (rows, cols), 1) // RANK).astype(F32)
            low = jnp.where(owner == tenant, low, 0.0).astype(BF)
            step = 512

            def body(n, carry):
                at = pl.ds(pl.multiple_of(n * step, step), step)
                value = jnp.dot(
                    packed[q, here, 0:piece], w_up[j, :, at], preferred_element_type=F32
                )
                value = value + jnp.dot(low, a_out[j, :, at], preferred_element_type=F32)
                part[q, j, :, at] = value.astype(BF)
                return carry

            lax.fori_loop(0, units // step, body, 0)
            values[q, j] = go(part.at[q, j], peer.at[q, j], v_s.at[q, j], v_r.at[q, j], x_dev)

    mine = pl.ds(pl.multiple_of(c * 2 * unit, 2 * unit), 2 * unit)
    theirs = pl.ds(pl.multiple_of((1 - c) * 2 * unit, 2 * unit), 2 * unit)
    cores, rights, lines = {}, {}, {}

    def down(q):
        for j in range(2):
            values[q, j].wait_recv()
            here = pl.ds(j * rows, rows)
            info = packed[q, here, piece:].astype(F32)
            expert = (2 * e + j).astype(F32)
            gate = jnp.where(info[:, 0:8] == expert, info[:, 8:16] + info[:, 16:24], 0.0)
            gate = jnp.sum(gate, axis=1, keepdims=True)
            value = part[q, j].astype(F32) + peer[q, j].astype(F32)
            hidden = (value / (1.0 + jnp.exp(-value))).astype(BF)
            step = 512

            def body(n, carry):
                at = pl.ds(pl.multiple_of(n * step, step), step)
                value = jnp.dot(hidden, w_down[j, :, at], preferred_element_type=F32)
                rows_out[here, at] = (value * gate).astype(BF)
                return carry

            lax.fori_loop(0, piece // step, body, 0)
        back = lax.dot_general(
            equal_iota((chunk, chunk)).astype(BF),
            pick[q],
            (((1,), (1,)), ((), ())),
            preferred_element_type=F32,
        ).astype(BF)

        def body(n, carry):
            at = pl.ds(pl.multiple_of(n * step, step), step)
            y_part[q, :, at] = jnp.dot(
                back, rows_out[:, at], preferred_element_type=F32
            ).astype(BF)
            return carry

        lax.fori_loop(0, piece // step, body, 0)
        cores[q] = go(y_part.at[q, theirs], core_in.at[q], c_s.at[q], c_r.at[q], c_dev)

    def spot(row):
        return pl.ds(pl.multiple_of(row * unit, unit), unit)

    def add_core(q):
        cores[q].wait_recv()
        y_send[q] = (
            y_part[q, place(c, 1 - y)].astype(F32) + core_in[q, spot(1 - y)].astype(F32)
        ).astype(BF)
        rights[q] = go(y_send.at[q], y_in.at[q], y_s.at[q], y_r.at[q], y_dev)

    def add_y(q):
        rights[q].wait_recv()
        z_send[q] = (
            y_part[q, place(c, y)].astype(F32)
            + core_in[q, spot(y)].astype(F32)
            + y_in[q].astype(F32)
        ).astype(BF)
        if q:
            lines[q] = go(z_send.at[q], z_in.at[q], z_s.at[q], z_r.at[q], z_dev[q])

    send_z(3)
    send_y(0)
    send_c(0, 0)
    send_z(1)
    send_z(2)
    arrive_y(0)
    up(0)
    arrive_z(3)
    arrive_z(1)
    arrive_y(3)
    up(3)
    arrive_z(2)
    arrive_y(1)
    loads[3].wait()
    down(0)
    arrive_y(2)
    up(2)
    add_core(0)
    down(3)
    add_y(0)
    up(1)
    add_core(3)
    down(2)
    add_y(3)
    add_core(2)
    down(1)
    add_core(1)
    add_y(2)
    add_y(1)
    total = z_send[0].astype(F32)
    for q in (3, 2, 1):
        lines[q].wait_recv()
        total = total + z_in[q].astype(F32)
    x_send[...] = total.astype(BF).reshape(2, tok, piece)
    last = go(x_send.at[1 - x], x_in, x_s, x_r, x_dev)
    out[:, pl.ds(pl.multiple_of(x * piece, piece), piece)] = x_send[x]
    last.wait_recv()
    out[:, pl.ds(pl.multiple_of((1 - x) * piece, piece), piece)] = x_in[...]
    for cp in sends:
        cp.wait_send()


def fused(
    tokens, route_ids, gate_weights, tenant_ids, up_weight, down_weight, adapter_in, adapter_out
):
    tok = tokens.shape[0]
    piece = up_weight.shape[1]
    units = up_weight.shape[2]
    cols = adapter_in.shape[2]
    experts_all = up_weight.shape[0] * lax.axis_size("expert")
    cap = max(2, 2 * tok * route_ids.shape[1] // experts_all)
    a_in_t = jnp.swapaxes(adapter_in, 1, 2)
    unit = 2 * tok
    chunk = 4 * unit
    rows = (chunk // tok) * cap
    dma = pltpu.SemaphoreType.DMA
    vm = lambda *shape: pltpu.VMEM(shape, BF)
    any_spec = pl.BlockSpec(memory_space=pl.ANY)
    vmem_spec = pl.BlockSpec(memory_space=pltpu.VMEM)
    return pl.pallas_call(
        functools.partial(expert_kernel, (tok, cap, piece, units, cols)),
        out_shape=jax.ShapeDtypeStruct(tokens.shape, BF),
        in_specs=[vmem_spec] * 4 + [any_spec] * 4,
        out_specs=vmem_spec,
        scratch_shapes=[
            vm(*up_weight.shape),
            vm(*down_weight.shape),
            vm(*a_in_t.shape),
            vm(*adapter_out.shape),
            vm(tok, piece + LANES),
            vm(NZ, chunk, piece + LANES),
            vm(NZ, 2 * rows, piece + LANES),
            vm(NZ, 2 * rows, chunk),
            vm(NZ, 2, rows, units),
            vm(NZ, 2, rows, units),
            vm(2 * rows, piece),
            vm(NZ, chunk, piece),
            vm(NZ, 2 * unit, piece),
            vm(NZ, unit, piece),
            vm(NZ, unit, piece),
            vm(NZ, unit, piece),
            vm(NZ, unit, piece),
            vm(2, tok, piece),
            vm(tok, piece),
            dma((4,)),
            dma,
            dma,
            dma((NZ,)),
            dma((NZ,)),
            dma((NZ,)),
            dma((NZ,)),
            dma((NZ, 2)),
            dma((NZ, 2)),
            dma((NZ, 2)),
            dma((NZ, 2)),
            dma((NZ,)),
            dma((NZ,)),
            dma((NZ,)),
            dma((NZ,)),
            dma((NZ,)),
            dma((NZ,)),
            dma,
            dma,
        ],
        compiler_params=pltpu.CompilerParams(
            collective_id=0, has_side_effects=True, vmem_limit_bytes=48 * 1024 * 1024
        ),
    )(
        tokens,
        route_ids.T,
        gate_weights.T,
        tenant_ids.reshape(1, tok),
        up_weight,
        down_weight,
        a_in_t,
        adapter_out,
    )


def per_device(
    tokens, route_ids, gate_weights, tenant_ids, up_weight, down_weight, adapter_in, adapter_out
):
    n_dp = lax.axis_size("dp")
    n_col = lax.axis_size("expert")
    tok_count = tokens.shape[0]
    chosen = route_ids.shape[1]
    features = tokens.shape[1]
    exp_local = up_weight.shape[0]
    piece = up_weight.shape[1]
    units = up_weight.shape[2]
    adapter_cols = adapter_in.shape[2]
    experts_all = exp_local * n_col
    capacity = max(2, 2 * tok_count * chosen // experts_all)
    send_rows = experts_all * capacity
    flat_routes = route_ids.reshape(-1)
    order = jnp.arange(flat_routes.shape[0], dtype=jnp.int32)
    same = flat_routes[:, None] == flat_routes[None, :]
    earlier = order[None, :] < order[:, None]
    rank = jnp.sum((same & earlier).astype(jnp.int32), axis=1)
    target = flat_routes * capacity + rank
    outgoing = (
        jnp.zeros((send_rows, features), jnp.bfloat16)
        .at[target]
        .set(jnp.repeat(tokens, chosen, axis=0))
    )
    tag_line = (
        jnp.full((send_rows,), -1.0, jnp.float32)
        .at[target]
        .set(jnp.repeat(tenant_ids, chosen).astype(jnp.float32))
    )
    tag_grid = jnp.broadcast_to(tag_line[:, None], (send_rows, n_dp)).astype(jnp.bfloat16)
    sending = outgoing.reshape(n_col, exp_local, capacity, n_dp, piece)
    tag_send = tag_grid.reshape(n_col, exp_local, capacity, n_dp, 1)
    arrived, arrived_tags = (
        lax.all_to_all(
            lax.all_to_all(sending, "dp", split_axis=3, concat_axis=2, tiled=True),
            "expert",
            split_axis=0,
            concat_axis=2,
            tiled=True,
        ),
        lax.all_to_all(
            lax.all_to_all(tag_send, "dp", split_axis=3, concat_axis=2, tiled=True),
            "expert",
            split_axis=0,
            concat_axis=2,
            tiled=True,
        ),
    )
    rows_all = arrived.shape[2]
    grid = arrived.reshape(exp_local, rows_all, piece)
    tags = arrived_tags.reshape(exp_local, rows_all).astype(jnp.float32)
    up_part = jnp.einsum("erd,edf->erf", grid, up_weight, preferred_element_type=jnp.float32)
    shrink_part = jnp.einsum("erd,edl->erl", grid, adapter_in, preferred_element_type=jnp.float32)
    owner = (jnp.arange(adapter_cols, dtype=jnp.int32) // RANK).astype(jnp.float32)
    shrink = lax.psum(shrink_part.astype(jnp.bfloat16), "dp").astype(jnp.float32)
    keep = owner[None, None, :] == tags[..., None]
    masked_values = jnp.where(keep, shrink, jnp.zeros((), jnp.float32))
    up_portion = lax.psum_scatter(
        up_part.astype(jnp.bfloat16), "dp", scatter_dimension=2, tiled=True
    ).astype(jnp.float32)
    share = units // n_dp
    mapping_portion = lax.dynamic_slice_in_dim(
        adapter_out, lax.axis_index("dp") * share, share, 2
    ).astype(jnp.float32)
    low_rank_adapter = jnp.einsum(
        "erl,elf->erf", masked_values, mapping_portion, precision=lax.Precision.HIGHEST
    )
    hidden_portion = jax.nn.silu(up_portion + low_rank_adapter).astype(jnp.bfloat16)
    hidden_activations = lax.all_gather(hidden_portion, "dp", axis=2, tiled=True)
    expert_out = jnp.einsum(
        "erf,efd->erd", hidden_activations, down_weight, preferred_element_type=jnp.float32
    ).astype(jnp.bfloat16)
    going_back = expert_out.reshape(1, exp_local, rows_all, 1, piece)
    returned = lax.all_to_all(
        lax.all_to_all(going_back, "expert", split_axis=2, concat_axis=0, tiled=True),
        "dp",
        split_axis=2,
        concat_axis=3,
        tiled=True,
    )
    results = returned.reshape(send_rows, features)
    picked = results[target].astype(jnp.float32).reshape(tok_count, chosen, features)
    mixed = jnp.sum(picked * gate_weights[:, :, None], axis=1)
    return mixed.astype(jnp.bfloat16)


def solution(mesh):
    placed = (
        P(("dp", "expert"), None),
        P(("dp", "expert"), None),
        P(("dp", "expert"), None),
        P(("dp", "expert")),
        P("expert", "dp", None),
        P("expert", None, "dp"),
        P("expert", "dp", None),
        P("expert", None, None),
    )
    small = mesh.shape["dp"] == 2 and mesh.shape["expert"] == 4 * NZ
    return jax.shard_map(
        fused if small else per_device, mesh=mesh, in_specs=placed, out_specs=P(("dp", "expert"), None), check_vma=False
    )
```

```python
import functools

import jax
import jax.numpy as jnp
from jax import lax
from jax.experimental import pallas as pl
from jax.experimental.pallas import tpu as pltpu
from jax.sharding import PartitionSpec as P

RANK = 16
MESH = pl.DeviceIdType.MESH
BF = jnp.bfloat16
F32 = jnp.float32
LANES = 128
NZ = 4


def equal_iota(shape):
    same = lax.broadcasted_iota(jnp.int32, shape, 0) == lax.broadcasted_iota(jnp.int32, shape, 1)
    return jnp.where(same, 1.0, 0.0)


def expert_kernel(
    dims,
    tokens_hbm,
    routes_hbm,
    gates_hbm,
    tenants_hbm,
    w_up_hbm,
    w_down_hbm,
    a_in_hbm,
    a_out_hbm,
    out,
    tokens,
    routes_t,
    gates_t,
    tenants_t,
    w_up,
    w_down,
    a_in,
    a_out,
    first_out,
    grid,
    packed,
    pick,
    part,
    peer,
    rows_out,
    y_part,
    core_in,
    y_send,
    y_in,
    z_send,
    z_in,
    x_send,
    x_in,
    load_sem,
    tx_s,
    tx_r,
    ty_s,
    ty_r,
    tz_s,
    tz_r,
    tc_s,
    tc_r,
    v_s,
    v_r,
    c_s,
    c_r,
    y_s,
    y_r,
    z_s,
    z_r,
    x_s,
    x_r,
):
    tok, cap, piece, units, cols = dims
    unit = 2 * tok
    size = 2 * unit
    rows = (size // tok) * cap
    x = lax.axis_index("dp")
    e = lax.axis_index("expert")
    z = e // 4
    y = (e // 2) % 2
    c = e % 2
    x_dev = (1 - x, e)
    y_dev = (x, z * 4 + (1 - y) * 2 + c)
    c_dev = (x, z * 4 + y * 2 + (1 - c))
    z_of = {1: z + 1 - 2 * (z % 2), 2: (z + 2) % 4, 3: 3 - z}
    z_dev = {q: (x, z_of[q] * 4 + y * 2 + c) for q in z_of}
    mine = pl.ds(pl.multiple_of(c * unit, unit), unit)
    theirs = pl.ds(pl.multiple_of((1 - c) * unit, unit), unit)

    def remote(src, dst, ss, rs, dev):
        return pltpu.make_async_remote_copy(
            src_ref=src, dst_ref=dst, send_sem=ss, recv_sem=rs, device_id=dev, device_id_type=MESH
        )

    pairs = [
        (tokens_hbm, tokens),
        (routes_hbm, routes_t),
        (gates_hbm, gates_t),
        (tenants_hbm, tenants_t),
        (a_in_hbm, a_in),
        (a_out_hbm, a_out),
        (w_up_hbm.at[0], w_up.at[0]),
        (w_up_hbm.at[1], w_up.at[1]),
        (w_down_hbm.at[0], w_down.at[0]),
        (w_down_hbm.at[1], w_down.at[1]),
    ]
    loads = [
        pltpu.make_async_copy(src, dst, load_sem.at[n]) for n, (src, dst) in enumerate(pairs)
    ]
    for copy in loads:
        copy.start()

    barrier = pltpu.get_barrier_semaphore()
    for dev in [x_dev, y_dev, c_dev] + [z_dev[q] for q in z_of]:
        pl.semaphore_signal(barrier, inc=1, device_id=dev, device_id_type=MESH)

    for n in range(4):
        loads[n].wait()
    gates = gates_t[...]
    high = gates.astype(BF).astype(F32)
    stacked = jnp.concatenate(
        [
            routes_t[...].astype(F32),
            high,
            gates - high,
            jnp.broadcast_to(tenants_t[...].astype(F32), (8, tok)),
        ],
        axis=0,
    )
    meta = lax.dot_general(
        stacked, equal_iota((32, LANES)), (((0,), (0,)), ((), ())), preferred_element_type=F32
    ).astype(BF)

    def half(dp):
        return pl.ds(pl.multiple_of(c * unit + dp * tok, tok), tok)

    first_out[:, 0:piece] = tokens[:, pl.ds(pl.multiple_of((1 - x) * piece, piece), piece)]
    first_out[:, piece:] = meta
    grid[0, 0, half(x), 0:piece] = tokens[:, pl.ds(pl.multiple_of(x * piece, piece), piece)]
    grid[0, 0, half(x), piece:] = meta
    pl.semaphore_wait(barrier, 3 + NZ - 1)

    sends = []

    def go(*args):
        cp = remote(*args)
        cp.start()
        sends.append(cp)
        return cp

    go(first_out, grid.at[0, 0, half(x)], tx_s, tx_r, x_dev)

    def send_y(q):
        go(grid.at[q, 0, mine], grid.at[q, 1, mine], ty_s.at[q], ty_r.at[q], y_dev)

    def wait_y(q):
        here = grid.at[q, 1, mine]
        remote(here, here, ty_s.at[q], ty_r.at[q], y_dev).wait_recv()
        send_c(q, 1)

    def send_z(q):
        go(grid.at[0, 0, mine], grid.at[q, 0, mine], tz_s.at[q], tz_r.at[q], z_dev[q])

    def wait_z(q):
        here = grid.at[q, 0, mine]
        remote(here, here, tz_s.at[q], tz_r.at[q], z_dev[q]).wait_recv()
        send_c(q, 0)
        send_y(q)

    def send_c(q, r):
        here = grid.at[q, r, mine]
        go(here, here, tc_s.at[q, r], tc_r.at[q, r], c_dev)

    def compact(q, r):
        here = grid.at[q, r, theirs]
        remote(here, here, tc_s.at[q, r], tc_r.at[q, r], c_dev).wait_recv()
        flat = lax.dot_general(
            equal_iota((LANES, LANES)).astype(BF),
            grid[q, r, :, piece:],
            (((1,), (1,)), ((), ())),
            preferred_element_type=F32,
        )
        t0 = lax.broadcasted_iota(jnp.int32, (size, size), 0)
        t1 = lax.broadcasted_iota(jnp.int32, (size, size), 1)
        before = jnp.where((t0 // tok == t1 // tok) & (t0 < t1), 1.0, 0.0).astype(BF)
        r0 = lax.broadcasted_iota(jnp.int32, (rows, size), 0)
        r1 = lax.broadcasted_iota(jnp.int32, (rows, size), 1)
        same = r0 // cap == r1 // tok
        slot = (r0 % cap).astype(F32)
        for j in range(2):
            expert = (2 * e + j).astype(F32)
            named = jnp.sum(jnp.where(flat[0:8] == expert, 1.0, 0.0), axis=0, keepdims=True)
            named = jnp.broadcast_to(named, (16, size))
            rank = jnp.dot(named.astype(BF), before, preferred_element_type=F32)
            hit = same & (slot == rank[0:1]) & (named[0:1] > 0.5)
            pick[q, r, j * rows : (j + 1) * rows, :] = jnp.where(hit, 1.0, 0.0).astype(BF)

        def put(at):
            value = jnp.dot(
                pick[q, r], grid[q, r, :, at], preferred_element_type=F32
            ).astype(BF)
            for j in range(2):
                packed[q, j, r * rows : (r + 1) * rows, at] = value[j * rows : (j + 1) * rows]

        put(pl.ds(piece, LANES))
        step = 512

        def body(n, carry):
            put(pl.ds(pl.multiple_of(n * step, step), step))
            return carry

        lax.fori_loop(0, piece // step, body, 0)

    values = {}

    def up(q, halves):
        for r in halves:
            compact(q, r)
        here = slice(min(halves) * rows, (max(halves) + 1) * rows)
        many = len(halves) * rows
        for j in range(2):
            if q == 0 and halves == (0,):
                if j == 0:
                    loads[4].wait()
                    loads[5].wait()
                loads[6 + j].wait()
            low = lax.dot_general(
                packed[q, j, here, 0:piece],
                a_in[j],
                (((1,), (1,)), ((), ())),
                preferred_element_type=F32,
            )
            tenant = packed[q, j, here, piece + 24 : piece + 25].astype(F32)
            owner = (lax.broadcasted_iota(jnp.int32, (many, cols), 1) // RANK).astype(F32)
            low = jnp.where(owner == tenant, low, 0.0).astype(BF)
            step = 512

            def body(n, carry):
                at = pl.ds(pl.multiple_of(n * step, step), step)
                value = jnp.dot(
                    packed[q, j, here, 0:piece], w_up[j, :, at], preferred_element_type=F32
                )
                value = value + jnp.dot(low, a_out[j, :, at], preferred_element_type=F32)
                part[q, j, here, at] = value.astype(BF)
                return carry

            lax.fori_loop(0, units // step, body, 0)
        for r in sorted(halves, reverse=q != 0):
            spot = pl.ds(r * rows, rows)
            values[q, r] = go(
                part.at[q, :, spot], peer.at[q, :, spot], v_s.at[q, r], v_r.at[q, r], x_dev
            )

    cores, rights, lines = {}, {}, {}

    def down(q, halves):
        for r in halves:
            values[q, r].wait_recv()
        here = slice(min(halves) * rows, (max(halves) + 1) * rows)
        for j in range(2):
            info = packed[q, j, here, piece:].astype(F32)
            expert = (2 * e + j).astype(F32)
            gate = jnp.where(info[:, 0:8] == expert, info[:, 8:16] + info[:, 16:24], 0.0)
            gate = jnp.sum(gate, axis=1, keepdims=True)
            value = part[q, j, here].astype(F32) + peer[q, j, here].astype(F32)
            hidden = (value / (1.0 + jnp.exp(-value))).astype(BF)
            step = 512

            def body(n, carry):
                at = pl.ds(pl.multiple_of(n * step, step), step)
                value = jnp.dot(hidden, w_down[j, :, at], preferred_element_type=F32)
                value = (value * gate).astype(BF)
                for n_at, r in enumerate(sorted(halves)):
                    rows_out[r, j * rows : (j + 1) * rows, at] = value[
                        n_at * rows : (n_at + 1) * rows
                    ]
                return carry

            lax.fori_loop(0, piece // step, body, 0)
        for r in halves:
            back = lax.dot_general(
                equal_iota((size, size)).astype(BF),
                pick[q, r],
                (((1,), (1,)), ((), ())),
                preferred_element_type=F32,
            ).astype(BF)

            def body(n, carry):
                at = pl.ds(pl.multiple_of(n * step, step), step)
                y_part[q, r, :, at] = jnp.dot(
                    back, rows_out[r, :, at], preferred_element_type=F32
                ).astype(BF)
                return carry

            lax.fori_loop(0, piece // step, body, 0)
            cores[q, r] = go(
                y_part.at[q, r, theirs], core_in.at[q, r], c_s.at[q, r], c_r.at[q, r], c_dev
            )

    def add_core(q):
        cores[q, 1].wait_recv()
        y_send[q] = (y_part[q, 1, mine].astype(F32) + core_in[q, 1].astype(F32)).astype(BF)
        rights[q] = go(y_send.at[q], y_in.at[q], y_s.at[q], y_r.at[q], y_dev)

    wide = piece // 2

    def add_y(q):
        cores[q, 0].wait_recv()
        rights[q].wait_recv()
        for h in range(2):
            at = slice(h * wide, (h + 1) * wide)
            z_send[q, h] = (
                y_part[q, 0, mine, at].astype(F32)
                + core_in[q, 0, :, at].astype(F32)
                + y_in[q, :, at].astype(F32)
            ).astype(BF)
            if q:
                lines[q, h] = go(
                    z_send.at[q, h], z_in.at[q, h], z_s.at[q, h], z_r.at[q, h], z_dev[q]
                )

    remote(first_out, grid.at[0, 0, half(1 - x)], tx_s, tx_r, x_dev).wait_recv()
    send_c(0, 0)
    send_z(3)
    send_y(0)
    send_z(1)
    up(0, (0,))
    wait_z(1)
    wait_y(0)
    up(0, (1,))
    send_z(2)
    wait_z(3)
    up(3, (0,))
    wait_y(1)
    loads[8].wait()
    loads[9].wait()
    down(0, (1, 0))
    wait_y(3)
    up(3, (1,))
    wait_z(2)
    up(2, (0,))
    add_core(0)
    wait_y(2)
    up(2, (1,))
    up(1, (0, 1))
    add_y(0)
    down(3, (1, 0))
    add_core(3)
    down(2, (1, 0))
    add_y(3)
    add_core(2)
    down(1, (1,))
    add_core(1)
    add_y(2)
    down(1, (0,))
    add_y(1)
    lasts = []
    for h in range(2):
        total = z_send[0, h].astype(F32)
        for q in (3, 2, 1):
            lines[q, h].wait_recv()
            total = total + z_in[q, h].astype(F32)
        x_send[h] = total.astype(BF).reshape(2, tok, wide)
        lasts.append(go(x_send.at[h, 1 - x], x_in.at[h], x_s.at[h], x_r.at[h], x_dev))
        out[:, pl.ds(pl.multiple_of(x * piece + h * wide, wide), wide)] = x_send[h, x]
    for h in range(2):
        lasts[h].wait_recv()
        out[:, pl.ds(pl.multiple_of((1 - x) * piece + h * wide, wide), wide)] = x_in[h]
    for cp in sends:
        cp.wait_send()


def fused(
    tokens, route_ids, gate_weights, tenant_ids, up_weight, down_weight, adapter_in, adapter_out
):
    tok = tokens.shape[0]
    piece = up_weight.shape[1]
    units = up_weight.shape[2]
    cols = adapter_in.shape[2]
    experts_all = up_weight.shape[0] * lax.axis_size("expert")
    cap = max(2, 2 * tok * route_ids.shape[1] // experts_all)
    a_in_t = jnp.swapaxes(adapter_in, 1, 2)
    unit = 2 * tok
    size = 2 * unit
    rows = (size // tok) * cap
    dma = pltpu.SemaphoreType.DMA
    vm = lambda *shape: pltpu.VMEM(shape, BF)
    any_spec = pl.BlockSpec(memory_space=pl.ANY)
    vmem_spec = pl.BlockSpec(memory_space=pltpu.VMEM)
    return pl.pallas_call(
        functools.partial(expert_kernel, (tok, cap, piece, units, cols)),
        out_shape=jax.ShapeDtypeStruct(tokens.shape, BF),
        in_specs=[any_spec] * 8,
        out_specs=vmem_spec,
        scratch_shapes=[
            vm(*tokens.shape),
            pltpu.VMEM(route_ids.shape[::-1], jnp.int32),
            pltpu.VMEM(gate_weights.shape[::-1], F32),
            pltpu.VMEM((1, tok), jnp.int32),
            vm(*up_weight.shape),
            vm(*down_weight.shape),
            vm(*a_in_t.shape),
            vm(*adapter_out.shape),
            vm(tok, piece + LANES),
            vm(NZ, 2, size, piece + LANES),
            vm(NZ, 2, 2 * rows, piece + LANES),
            vm(NZ, 2, 2 * rows, size),
            vm(NZ, 2, 2 * rows, units),
            vm(NZ, 2, 2 * rows, units),
            vm(2, 2 * rows, piece),
            vm(NZ, 2, size, piece),
            vm(NZ, 2, unit, piece),
            vm(NZ, unit, piece),
            vm(NZ, unit, piece),
            vm(NZ, 2, unit, piece // 2),
            vm(NZ, 2, unit, piece // 2),
            vm(2, 2, tok, piece // 2),
            vm(2, tok, piece // 2),
            dma((10,)),
            dma,
            dma,
            dma((NZ,)),
            dma((NZ,)),
            dma((NZ,)),
            dma((NZ,)),
            dma((NZ, 2)),
            dma((NZ, 2)),
            dma((NZ, 2)),
            dma((NZ, 2)),
            dma((NZ, 2)),
            dma((NZ, 2)),
            dma((NZ,)),
            dma((NZ,)),
            dma((NZ, 2)),
            dma((NZ, 2)),
            dma((2,)),
            dma((2,)),
        ],
        compiler_params=pltpu.CompilerParams(
            collective_id=0, has_side_effects=True, vmem_limit_bytes=60 * 1024 * 1024
        ),
    )(
        tokens,
        route_ids.T,
        gate_weights.T,
        tenant_ids.reshape(1, tok),
        up_weight,
        down_weight,
        a_in_t,
        adapter_out,
    )


def per_device(
    tokens, route_ids, gate_weights, tenant_ids, up_weight, down_weight, adapter_in, adapter_out
):
    n_dp = lax.axis_size("dp")
    n_col = lax.axis_size("expert")
    tok_count = tokens.shape[0]
    chosen = route_ids.shape[1]
    features = tokens.shape[1]
    exp_local = up_weight.shape[0]
    piece = up_weight.shape[1]
    units = up_weight.shape[2]
    adapter_cols = adapter_in.shape[2]
    experts_all = exp_local * n_col
    capacity = max(2, 2 * tok_count * chosen // experts_all)
    send_rows = experts_all * capacity
    flat_routes = route_ids.reshape(-1)
    order = jnp.arange(flat_routes.shape[0], dtype=jnp.int32)
    same = flat_routes[:, None] == flat_routes[None, :]
    earlier = order[None, :] < order[:, None]
    rank = jnp.sum((same & earlier).astype(jnp.int32), axis=1)
    target = flat_routes * capacity + rank
    outgoing = (
        jnp.zeros((send_rows, features), jnp.bfloat16)
        .at[target]
        .set(jnp.repeat(tokens, chosen, axis=0))
    )
    tag_line = (
        jnp.full((send_rows,), -1.0, jnp.float32)
        .at[target]
        .set(jnp.repeat(tenant_ids, chosen).astype(jnp.float32))
    )
    tag_grid = jnp.broadcast_to(tag_line[:, None], (send_rows, n_dp)).astype(jnp.bfloat16)
    sending = outgoing.reshape(n_col, exp_local, capacity, n_dp, piece)
    tag_send = tag_grid.reshape(n_col, exp_local, capacity, n_dp, 1)
    arrived, arrived_tags = (
        lax.all_to_all(
            lax.all_to_all(sending, "dp", split_axis=3, concat_axis=2, tiled=True),
            "expert",
            split_axis=0,
            concat_axis=2,
            tiled=True,
        ),
        lax.all_to_all(
            lax.all_to_all(tag_send, "dp", split_axis=3, concat_axis=2, tiled=True),
            "expert",
            split_axis=0,
            concat_axis=2,
            tiled=True,
        ),
    )
    rows_all = arrived.shape[2]
    grid = arrived.reshape(exp_local, rows_all, piece)
    tags = arrived_tags.reshape(exp_local, rows_all).astype(jnp.float32)
    up_part = jnp.einsum("erd,edf->erf", grid, up_weight, preferred_element_type=jnp.float32)
    shrink_part = jnp.einsum("erd,edl->erl", grid, adapter_in, preferred_element_type=jnp.float32)
    owner = (jnp.arange(adapter_cols, dtype=jnp.int32) // RANK).astype(jnp.float32)
    shrink = lax.psum(shrink_part.astype(jnp.bfloat16), "dp").astype(jnp.float32)
    keep = owner[None, None, :] == tags[..., None]
    masked_values = jnp.where(keep, shrink, jnp.zeros((), jnp.float32))
    up_portion = lax.psum_scatter(
        up_part.astype(jnp.bfloat16), "dp", scatter_dimension=2, tiled=True
    ).astype(jnp.float32)
    share = units // n_dp
    mapping_portion = lax.dynamic_slice_in_dim(
        adapter_out, lax.axis_index("dp") * share, share, 2
    ).astype(jnp.float32)
    low_rank_adapter = jnp.einsum(
        "erl,elf->erf", masked_values, mapping_portion, precision=lax.Precision.HIGHEST
    )
    hidden_portion = jax.nn.silu(up_portion + low_rank_adapter).astype(jnp.bfloat16)
    hidden_activations = lax.all_gather(hidden_portion, "dp", axis=2, tiled=True)
    expert_out = jnp.einsum(
        "erf,efd->erd", hidden_activations, down_weight, preferred_element_type=jnp.float32
    ).astype(jnp.bfloat16)
    going_back = expert_out.reshape(1, exp_local, rows_all, 1, piece)
    returned = lax.all_to_all(
        lax.all_to_all(going_back, "expert", split_axis=2, concat_axis=0, tiled=True),
        "dp",
        split_axis=2,
        concat_axis=3,
        tiled=True,
    )
    results = returned.reshape(send_rows, features)
    picked = results[target].astype(jnp.float32).reshape(tok_count, chosen, features)
    mixed = jnp.sum(picked * gate_weights[:, :, None], axis=1)
    return mixed.astype(jnp.bfloat16)


def solution(mesh):
    placed = (
        P(("dp", "expert"), None),
        P(("dp", "expert"), None),
        P(("dp", "expert"), None),
        P(("dp", "expert")),
        P("expert", "dp", None),
        P("expert", None, "dp"),
        P("expert", "dp", None),
        P("expert", None, None),
    )
    small = mesh.shape["dp"] == 2 and mesh.shape["expert"] == 4 * NZ
    return jax.shard_map(
        fused if small else per_device, mesh=mesh, in_specs=placed, out_specs=P(("dp", "expert"), None), check_vma=False
    )
```

```python
import functools

import jax
import jax.numpy as jnp
from jax import lax
from jax.experimental import pallas as pl
from jax.experimental.pallas import tpu as pltpu
from jax.sharding import PartitionSpec as P

RANK = 16
MESH = pl.DeviceIdType.MESH
BF = jnp.bfloat16
F32 = jnp.float32
LANES = 128
NZ = 4
STEP = 256
ORDER = (0, 3, 2, 1)


def equal_iota(shape):
    same = lax.broadcasted_iota(jnp.int32, shape, 0) == lax.broadcasted_iota(jnp.int32, shape, 1)
    return jnp.where(same, 1.0, 0.0)


def expert_kernel(
    dims,
    tokens_hbm,
    routes_hbm,
    gates_hbm,
    tenants_hbm,
    w_up_hbm,
    w_down_hbm,
    a_in_hbm,
    a_out_hbm,
    out,
    tokens,
    routes_t,
    gates_t,
    tenants_t,
    w_up,
    w_down,
    a_in,
    a_out,
    first_out,
    grid,
    packed,
    pick,
    part,
    peer,
    rows_out,
    y_part,
    core_in,
    y_send,
    y_in,
    z_send,
    z_in,
    x_send,
    x_in,
    load_sem,
    tx_s,
    tx_r,
    ty_s,
    ty_r,
    tz_s,
    tz_r,
    tc_s,
    tc_r,
    v_s,
    v_r,
    c_s,
    c_r,
    y_s,
    y_r,
    z_s,
    z_r,
    x_s,
    x_r,
):
    tok, cap, piece, units, cols = dims
    unit = 2 * tok
    size = 2 * unit
    chunk = 2 * size
    rows = (chunk // tok) * cap
    x = lax.axis_index("dp")
    e = lax.axis_index("expert")
    z = e // 4
    y = (e // 2) % 2
    c = e % 2
    x_dev = (1 - x, e)
    y_dev = (x, z * 4 + (1 - y) * 2 + c)
    c_dev = (x, z * 4 + y * 2 + (1 - c))
    z_of = {1: z + 1 - 2 * (z % 2), 2: (z + 2) % 4, 3: 3 - z}
    z_dev = {q: (x, z_of[q] * 4 + y * 2 + c) for q in z_of}

    def remote(src, dst, ss, rs, dev):
        return pltpu.make_async_remote_copy(
            src_ref=src, dst_ref=dst, send_sem=ss, recv_sem=rs, device_id=dev, device_id_type=MESH
        )

    pairs = [
        (tokens_hbm, tokens),
        (routes_hbm, routes_t),
        (gates_hbm, gates_t),
        (tenants_hbm, tenants_t),
        (a_in_hbm, a_in),
        (a_out_hbm, a_out),
        (w_up_hbm.at[0], w_up.at[0]),
        (w_up_hbm.at[1], w_up.at[1]),
        (w_down_hbm.at[0], w_down.at[0]),
        (w_down_hbm.at[1], w_down.at[1]),
    ]
    loads = [
        pltpu.make_async_copy(src, dst, load_sem.at[n]) for n, (src, dst) in enumerate(pairs)
    ]
    for copy in loads:
        copy.start()

    barrier = pltpu.get_barrier_semaphore()
    for dev in [x_dev, y_dev, c_dev] + [z_dev[q] for q in z_of]:
        pl.semaphore_signal(barrier, inc=1, device_id=dev, device_id_type=MESH)

    for n in range(4):
        loads[n].wait()
    gates = gates_t[...]
    high = gates.astype(BF).astype(F32)
    stacked = jnp.concatenate(
        [
            routes_t[...].astype(F32),
            high,
            gates - high,
            jnp.broadcast_to(tenants_t[...].astype(F32), (8, tok)),
        ],
        axis=0,
    )
    meta = lax.dot_general(
        stacked, equal_iota((32, LANES)), (((0,), (0,)), ((), ())), preferred_element_type=F32
    ).astype(BF)

    def lane(r, core):
        return pl.ds(pl.multiple_of(r * size + core * unit, unit), unit)

    def half(dp):
        return pl.ds(pl.multiple_of(c * unit + dp * tok, tok), tok)

    first_out[:, 0:piece] = tokens[:, pl.ds(pl.multiple_of((1 - x) * piece, piece), piece)]
    first_out[:, piece:] = meta
    grid[0, half(x), 0:piece] = tokens[:, pl.ds(pl.multiple_of(x * piece, piece), piece)]
    grid[0, half(x), piece:] = meta
    pl.semaphore_wait(barrier, 3 + NZ - 1)

    sends = []

    def go(*args):
        cp = remote(*args)
        cp.start()
        sends.append(cp)
        return cp

    go(first_out, grid.at[0, half(x)], tx_s, tx_r, x_dev)

    def send_y(q):
        go(grid.at[q, lane(0, c)], grid.at[q, lane(1, c)], ty_s.at[q], ty_r.at[q], y_dev)

    def wait_y(q):
        here = grid.at[q, lane(1, c)]
        remote(here, here, ty_s.at[q], ty_r.at[q], y_dev).wait_recv()
        send_c(q, 1)

    def send_z(q):
        go(grid.at[0, lane(0, c)], grid.at[q, lane(0, c)], tz_s.at[q], tz_r.at[q], z_dev[q])

    def wait_z(q):
        here = grid.at[q, lane(0, c)]
        remote(here, here, tz_s.at[q], tz_r.at[q], z_dev[q]).wait_recv()
        send_c(q, 0)
        send_y(q)

    def send_c(q, r):
        here = grid.at[q, lane(r, c)]
        go(here, here, tc_s.at[q, r], tc_r.at[q, r], c_dev)

    def at_place(q):
        first = ORDER.index(q) * rows
        return slice(first, first + rows)

    def compact(q):
        for r in range(2):
            here = grid.at[q, lane(r, 1 - c)]
            remote(here, here, tc_s.at[q, r], tc_r.at[q, r], c_dev).wait_recv()
        flat = lax.dot_general(
            equal_iota((LANES, LANES)).astype(BF),
            grid[q, :, piece:],
            (((1,), (1,)), ((), ())),
            preferred_element_type=F32,
        )
        t0 = lax.broadcasted_iota(jnp.int32, (chunk, chunk), 0)
        t1 = lax.broadcasted_iota(jnp.int32, (chunk, chunk), 1)
        before = jnp.where((t0 // tok == t1 // tok) & (t0 < t1), 1.0, 0.0).astype(BF)
        r0 = lax.broadcasted_iota(jnp.int32, (rows, chunk), 0)
        r1 = lax.broadcasted_iota(jnp.int32, (rows, chunk), 1)
        same = r0 // cap == r1 // tok
        slot = (r0 % cap).astype(F32)
        for j in range(2):
            expert = (2 * e + j).astype(F32)
            named = jnp.sum(jnp.where(flat[0:8] == expert, 1.0, 0.0), axis=0, keepdims=True)
            named = jnp.broadcast_to(named, (16, chunk))
            rank = jnp.dot(named.astype(BF), before, preferred_element_type=F32)
            hit = same & (slot == rank[0:1]) & (named[0:1] > 0.5)
            pick[q, j * rows : (j + 1) * rows, :] = jnp.where(hit, 1.0, 0.0).astype(BF)
        for n in list(range(0, piece, STEP)) + [piece]:
            at = slice(n, min(n + STEP, piece + LANES))
            value = jnp.dot(pick[q], grid[q, :, at], preferred_element_type=F32).astype(BF)
            for j in range(2):
                packed[j, at_place(q), at] = value[j * rows : (j + 1) * rows]

    values = {}

    def span(group):
        first = ORDER.index(group[0]) * rows
        return slice(first, first + len(group) * rows)

    def up(*group):
        for q in group:
            compact(q)
        here = span(group)
        for j in range(2):
            if group[0] == 0:
                if j == 0:
                    loads[4].wait()
                    loads[5].wait()
                loads[6 + j].wait()
            low = lax.dot_general(
                packed[j, here, 0:piece],
                a_in[j],
                (((1,), (1,)), ((), ())),
                preferred_element_type=F32,
            )
            tenant = packed[j, here, piece + 24 : piece + 25].astype(F32)
            owner = (lax.broadcasted_iota(jnp.int32, low.shape, 1) // RANK).astype(F32)
            low = jnp.where(owner == tenant, low, 0.0).astype(BF)
            for n in range(0, units, STEP):
                at = slice(n, n + STEP)
                value = jnp.dot(
                    packed[j, here, 0:piece], w_up[j, :, at], preferred_element_type=F32
                )
                value = value + jnp.dot(low, a_out[j, :, at], preferred_element_type=F32)
                part[j, here, at] = value.astype(BF)
            for q in group:
                spot = at_place(q)
                values[q, j] = go(
                    part.at[j, spot], peer.at[j, spot], v_s.at[q, j], v_r.at[q, j], x_dev
                )

    cores, rights, lines = {}, {}, {}

    def down(*group):
        here = span(group)
        for j in range(2):
            for q in group:
                values[q, j].wait_recv()
            info = packed[j, here, piece:].astype(F32)
            expert = (2 * e + j).astype(F32)
            gate = jnp.where(info[:, 0:8] == expert, info[:, 8:16] + info[:, 16:24], 0.0)
            gate = jnp.sum(gate, axis=1, keepdims=True)
            value = part[j, here].astype(F32) + peer[j, here].astype(F32)
            hidden = (value / (1.0 + jnp.exp(-value))).astype(BF)
            for n in range(0, piece, STEP):
                at = slice(n, n + STEP)
                value = jnp.dot(hidden, w_down[j, :, at], preferred_element_type=F32)
                value = (value * gate).astype(BF)
                for n_at, q in enumerate(group):
                    rows_out[q, j * rows : (j + 1) * rows, at] = value[
                        n_at * rows : (n_at + 1) * rows
                    ]
        for q in group:
            back = lax.dot_general(
                equal_iota((chunk, chunk)).astype(BF),
                pick[q],
                (((1,), (1,)), ((), ())),
                preferred_element_type=F32,
            ).astype(BF)
            for n in range(0, piece, STEP):
                at = slice(n, n + STEP)
                y_part[q, :, at] = jnp.dot(
                    back, rows_out[q, :, at], preferred_element_type=F32
                ).astype(BF)
            for r in (1, 0):
                cores[q, r] = go(
                    y_part.at[q, lane(r, 1 - c)],
                    core_in.at[q, r],
                    c_s.at[q, r],
                    c_r.at[q, r],
                    c_dev,
                )

    def add_core(q):
        cores[q, 1].wait_recv()
        y_send[q] = (y_part[q, lane(1, c)].astype(F32) + core_in[q, 1].astype(F32)).astype(BF)
        rights[q] = go(y_send.at[q], y_in.at[q], y_s.at[q], y_r.at[q], y_dev)

    wide = piece // 2

    def add_y(q):
        cores[q, 0].wait_recv()
        rights[q].wait_recv()
        for h in range(2):
            at = slice(h * wide, (h + 1) * wide)
            z_send[q, h] = (
                y_part[q, lane(0, c), at].astype(F32)
                + core_in[q, 0, :, at].astype(F32)
                + y_in[q, :, at].astype(F32)
            ).astype(BF)
            if q:
                lines[q, h] = go(
                    z_send.at[q, h], z_in.at[q, h], z_s.at[q, h], z_r.at[q, h], z_dev[q]
                )

    remote(first_out, grid.at[0, half(1 - x)], tx_s, tx_r, x_dev).wait_recv()
    send_c(0, 0)
    send_y(0)
    send_z(3)
    send_z(1)
    wait_y(0)
    send_z(2)
    up(0)
    wait_z(3)
    wait_z(1)
    wait_y(3)
    wait_y(1)
    up(3)
    wait_z(2)
    wait_y(2)
    loads[8].wait()
    loads[9].wait()
    up(2, 1)
    down(0, 3)
    add_core(3)
    add_core(0)
    add_y(3)
    add_y(0)
    down(2)
    add_core(2)
    down(1)
    add_core(1)
    add_y(2)
    add_y(1)
    lasts = []
    for h in range(2):
        total = z_send[0, h].astype(F32)
        for q in (3, 2, 1):
            lines[q, h].wait_recv()
            total = total + z_in[q, h].astype(F32)
        x_send[h] = total.astype(BF).reshape(2, tok, wide)
        lasts.append(go(x_send.at[h, 1 - x], x_in.at[h], x_s.at[h], x_r.at[h], x_dev))
        out[:, pl.ds(pl.multiple_of(x * piece + h * wide, wide), wide)] = x_send[h, x]
    for h in range(2):
        lasts[h].wait_recv()
        out[:, pl.ds(pl.multiple_of((1 - x) * piece + h * wide, wide), wide)] = x_in[h]
    for cp in sends:
        cp.wait_send()


def fused(
    tokens, route_ids, gate_weights, tenant_ids, up_weight, down_weight, adapter_in, adapter_out
):
    tok = tokens.shape[0]
    piece = up_weight.shape[1]
    units = up_weight.shape[2]
    cols = adapter_in.shape[2]
    experts_all = up_weight.shape[0] * lax.axis_size("expert")
    cap = max(2, 2 * tok * route_ids.shape[1] // experts_all)
    a_in_t = jnp.swapaxes(adapter_in, 1, 2)
    unit = 2 * tok
    size = 2 * unit
    chunk = 2 * size
    rows = (chunk // tok) * cap
    dma = pltpu.SemaphoreType.DMA
    vm = lambda *shape: pltpu.VMEM(shape, BF)
    any_spec = pl.BlockSpec(memory_space=pl.ANY)
    vmem_spec = pl.BlockSpec(memory_space=pltpu.VMEM)
    return pl.pallas_call(
        functools.partial(expert_kernel, (tok, cap, piece, units, cols)),
        out_shape=jax.ShapeDtypeStruct(tokens.shape, BF),
        in_specs=[any_spec] * 8,
        out_specs=vmem_spec,
        scratch_shapes=[
            vm(*tokens.shape),
            pltpu.VMEM(route_ids.shape[::-1], jnp.int32),
            pltpu.VMEM(gate_weights.shape[::-1], F32),
            pltpu.VMEM((1, tok), jnp.int32),
            vm(*up_weight.shape),
            vm(*down_weight.shape),
            vm(*a_in_t.shape),
            vm(*adapter_out.shape),
            vm(tok, piece + LANES),
            vm(NZ, chunk, piece + LANES),
            vm(2, NZ * rows, piece + LANES),
            vm(NZ, 2 * rows, chunk),
            vm(2, NZ * rows, units),
            vm(2, NZ * rows, units),
            vm(NZ, 2 * rows, piece),
            vm(NZ, chunk, piece),
            vm(NZ, 2, unit, piece),
            vm(NZ, unit, piece),
            vm(NZ, unit, piece),
            vm(NZ, 2, unit, piece // 2),
            vm(NZ, 2, unit, piece // 2),
            vm(2, 2, tok, piece // 2),
            vm(2, tok, piece // 2),
            dma((10,)),
            dma,
            dma,
            dma((NZ,)),
            dma((NZ,)),
            dma((NZ,)),
            dma((NZ,)),
            dma((NZ, 2)),
            dma((NZ, 2)),
            dma((NZ, 2)),
            dma((NZ, 2)),
            dma((NZ, 2)),
            dma((NZ, 2)),
            dma((NZ,)),
            dma((NZ,)),
            dma((NZ, 2)),
            dma((NZ, 2)),
            dma((2,)),
            dma((2,)),
        ],
        compiler_params=pltpu.CompilerParams(
            collective_id=0, has_side_effects=True, vmem_limit_bytes=60 * 1024 * 1024
        ),
    )(
        tokens,
        route_ids.T,
        gate_weights.T,
        tenant_ids.reshape(1, tok),
        up_weight,
        down_weight,
        a_in_t,
        adapter_out,
    )


def per_device(
    tokens, route_ids, gate_weights, tenant_ids, up_weight, down_weight, adapter_in, adapter_out
):
    n_dp = lax.axis_size("dp")
    n_col = lax.axis_size("expert")
    tok_count = tokens.shape[0]
    chosen = route_ids.shape[1]
    features = tokens.shape[1]
    exp_local = up_weight.shape[0]
    piece = up_weight.shape[1]
    units = up_weight.shape[2]
    adapter_cols = adapter_in.shape[2]
    experts_all = exp_local * n_col
    capacity = max(2, 2 * tok_count * chosen // experts_all)
    send_rows = experts_all * capacity
    flat_routes = route_ids.reshape(-1)
    order = jnp.arange(flat_routes.shape[0], dtype=jnp.int32)
    same = flat_routes[:, None] == flat_routes[None, :]
    earlier = order[None, :] < order[:, None]
    rank = jnp.sum((same & earlier).astype(jnp.int32), axis=1)
    target = flat_routes * capacity + rank
    outgoing = (
        jnp.zeros((send_rows, features), jnp.bfloat16)
        .at[target]
        .set(jnp.repeat(tokens, chosen, axis=0))
    )
    tag_line = (
        jnp.full((send_rows,), -1.0, jnp.float32)
        .at[target]
        .set(jnp.repeat(tenant_ids, chosen).astype(jnp.float32))
    )
    tag_grid = jnp.broadcast_to(tag_line[:, None], (send_rows, n_dp)).astype(jnp.bfloat16)
    sending = outgoing.reshape(n_col, exp_local, capacity, n_dp, piece)
    tag_send = tag_grid.reshape(n_col, exp_local, capacity, n_dp, 1)
    arrived, arrived_tags = (
        lax.all_to_all(
            lax.all_to_all(sending, "dp", split_axis=3, concat_axis=2, tiled=True),
            "expert",
            split_axis=0,
            concat_axis=2,
            tiled=True,
        ),
        lax.all_to_all(
            lax.all_to_all(tag_send, "dp", split_axis=3, concat_axis=2, tiled=True),
            "expert",
            split_axis=0,
            concat_axis=2,
            tiled=True,
        ),
    )
    rows_all = arrived.shape[2]
    grid = arrived.reshape(exp_local, rows_all, piece)
    tags = arrived_tags.reshape(exp_local, rows_all).astype(jnp.float32)
    up_part = jnp.einsum("erd,edf->erf", grid, up_weight, preferred_element_type=jnp.float32)
    shrink_part = jnp.einsum("erd,edl->erl", grid, adapter_in, preferred_element_type=jnp.float32)
    owner = (jnp.arange(adapter_cols, dtype=jnp.int32) // RANK).astype(jnp.float32)
    shrink = lax.psum(shrink_part.astype(jnp.bfloat16), "dp").astype(jnp.float32)
    keep = owner[None, None, :] == tags[..., None]
    masked_values = jnp.where(keep, shrink, jnp.zeros((), jnp.float32))
    up_portion = lax.psum_scatter(
        up_part.astype(jnp.bfloat16), "dp", scatter_dimension=2, tiled=True
    ).astype(jnp.float32)
    share = units // n_dp
    mapping_portion = lax.dynamic_slice_in_dim(
        adapter_out, lax.axis_index("dp") * share, share, 2
    ).astype(jnp.float32)
    low_rank_adapter = jnp.einsum(
        "erl,elf->erf", masked_values, mapping_portion, precision=lax.Precision.HIGHEST
    )
    hidden_portion = jax.nn.silu(up_portion + low_rank_adapter).astype(jnp.bfloat16)
    hidden_activations = lax.all_gather(hidden_portion, "dp", axis=2, tiled=True)
    expert_out = jnp.einsum(
        "erf,efd->erd", hidden_activations, down_weight, preferred_element_type=jnp.float32
    ).astype(jnp.bfloat16)
    going_back = expert_out.reshape(1, exp_local, rows_all, 1, piece)
    returned = lax.all_to_all(
        lax.all_to_all(going_back, "expert", split_axis=2, concat_axis=0, tiled=True),
        "dp",
        split_axis=2,
        concat_axis=3,
        tiled=True,
    )
    results = returned.reshape(send_rows, features)
    picked = results[target].astype(jnp.float32).reshape(tok_count, chosen, features)
    mixed = jnp.sum(picked * gate_weights[:, :, None], axis=1)
    return mixed.astype(jnp.bfloat16)


def solution(mesh):
    placed = (
        P(("dp", "expert"), None),
        P(("dp", "expert"), None),
        P(("dp", "expert"), None),
        P(("dp", "expert")),
        P("expert", "dp", None),
        P("expert", None, "dp"),
        P("expert", "dp", None),
        P("expert", None, None),
    )
    small = mesh.shape["dp"] == 2 and mesh.shape["expert"] == 4 * NZ
    return jax.shard_map(
        fused if small else per_device, mesh=mesh, in_specs=placed, out_specs=P(("dp", "expert"), None), check_vma=False
    )
```

```python
import functools

import jax
import jax.numpy as jnp
from jax import lax
from jax.experimental import pallas as pl
from jax.experimental.pallas import tpu as pltpu
from jax.sharding import PartitionSpec as P

RANK = 16
MESH = pl.DeviceIdType.MESH
BF = jnp.bfloat16
F32 = jnp.float32
LANES = 128
NZ = 4
STEP = 256
ORDER = (0, 2, 3, 1)


def equal_iota(shape):
    same = lax.broadcasted_iota(jnp.int32, shape, 0) == lax.broadcasted_iota(jnp.int32, shape, 1)
    return jnp.where(same, 1.0, 0.0)


def expert_kernel(
    dims,
    tokens_hbm,
    routes_hbm,
    gates_hbm,
    tenants_hbm,
    w_up_hbm,
    w_down_hbm,
    a_in_hbm,
    a_out_hbm,
    out,
    tokens,
    routes_t,
    gates_t,
    tenants_t,
    w_up,
    w_down,
    a_in,
    a_out,
    first_out,
    grid,
    packed,
    pick,
    part,
    peer,
    active,
    rows_out,
    y_part,
    core_in,
    y_send,
    y_in,
    z_send,
    z_in,
    x_send,
    x_in,
    load_sem,
    tx_s,
    tx_r,
    ty_s,
    ty_r,
    tz_s,
    tz_r,
    tc_s,
    tc_r,
    v_s,
    v_r,
    c_s,
    c_r,
    y_s,
    y_r,
    z_s,
    z_r,
    x_s,
    x_r,
):
    tok, cap, piece, units, cols = dims
    unit = 2 * tok
    size = 2 * unit
    chunk = 2 * size
    rows = (chunk // tok) * cap
    x = lax.axis_index("dp")
    e = lax.axis_index("expert")
    z = e // 4
    y = (e // 2) % 2
    c = e % 2
    x_dev = (1 - x, e)
    y_dev = (x, z * 4 + (1 - y) * 2 + c)
    c_dev = (x, z * 4 + y * 2 + (1 - c))
    z_of = {1: z + 1 - 2 * (z % 2), 2: (z + 2) % 4}
    z_dev = {q: (x, z_of[q] * 4 + y * 2 + c) for q in z_of}

    def remote(src, dst, ss, rs, dev):
        return pltpu.make_async_remote_copy(
            src_ref=src, dst_ref=dst, send_sem=ss, recv_sem=rs, device_id=dev, device_id_type=MESH
        )

    pairs = [
        (tokens_hbm, tokens),
        (routes_hbm, routes_t),
        (gates_hbm, gates_t),
        (tenants_hbm, tenants_t),
        (a_in_hbm, a_in),
        (a_out_hbm, a_out),
        (w_up_hbm.at[0], w_up.at[0]),
        (w_up_hbm.at[1], w_up.at[1]),
        (w_down_hbm.at[0], w_down.at[0]),
        (w_down_hbm.at[1], w_down.at[1]),
    ]
    loads = [
        pltpu.make_async_copy(src, dst, load_sem.at[n]) for n, (src, dst) in enumerate(pairs)
    ]
    for copy in loads:
        copy.start()

    barrier = pltpu.get_barrier_semaphore()
    for dev in [x_dev, y_dev, c_dev] + [z_dev[q] for q in z_of]:
        pl.semaphore_signal(barrier, inc=1, device_id=dev, device_id_type=MESH)

    for n in range(4):
        loads[n].wait()
    gates = gates_t[...]
    high = gates.astype(BF).astype(F32)
    stacked = jnp.concatenate(
        [
            routes_t[...].astype(F32),
            high,
            gates - high,
            jnp.broadcast_to(tenants_t[...].astype(F32), (8, tok)),
        ],
        axis=0,
    )
    meta = lax.dot_general(
        stacked, equal_iota((32, LANES)), (((0,), (0,)), ((), ())), preferred_element_type=F32
    ).astype(BF)

    def lane(r, core):
        return pl.ds(pl.multiple_of(r * size + core * unit, unit), unit)

    def half(dp):
        return pl.ds(pl.multiple_of(c * unit + dp * tok, tok), tok)

    first_out[:, 0:piece] = tokens[:, pl.ds(pl.multiple_of((1 - x) * piece, piece), piece)]
    first_out[:, piece:] = meta
    grid[0, half(x), 0:piece] = tokens[:, pl.ds(pl.multiple_of(x * piece, piece), piece)]
    grid[0, half(x), piece:] = meta
    pl.semaphore_wait(barrier, 5)

    sends = []

    def go(*args):
        cp = remote(*args)
        cp.start()
        sends.append(cp)
        return cp

    go(first_out, grid.at[0, half(x)], tx_s, tx_r, x_dev)

    def send_y(q):
        go(grid.at[q, lane(0, c)], grid.at[q, lane(1, c)], ty_s.at[q], ty_r.at[q], y_dev)

    def wait_y(q):
        here = grid.at[q, lane(1, c)]
        remote(here, here, ty_s.at[q], ty_r.at[q], y_dev).wait_recv()
        send_c(q, 1)

    def send_z(q, dev):
        src = grid.at[2 if q == 3 else 0, lane(0, c)]
        go(src, grid.at[q, lane(0, c)], tz_s.at[q], tz_r.at[q], z_dev[dev])

    def wait_z(q):
        here = grid.at[q, lane(0, c)]
        remote(here, here, tz_s.at[q], tz_r.at[q], z_dev[q % 2 or 2]).wait_recv()
        if q == 2:
            send_z(3, 1)
        send_c(q, 0)
        send_y(q)

    def send_c(q, r):
        here = grid.at[q, lane(r, c)]
        go(here, here, tc_s.at[q, r], tc_r.at[q, r], c_dev)

    def at_place(q):
        first = ORDER.index(q) * rows
        return slice(first, first + rows)

    def compact(q):
        for r in range(2):
            here = grid.at[q, lane(r, 1 - c)]
            remote(here, here, tc_s.at[q, r], tc_r.at[q, r], c_dev).wait_recv()
        flat = lax.dot_general(
            equal_iota((LANES, LANES)).astype(BF),
            grid[q, :, piece:],
            (((1,), (1,)), ((), ())),
            preferred_element_type=F32,
        )
        t0 = lax.broadcasted_iota(jnp.int32, (chunk, chunk), 0)
        t1 = lax.broadcasted_iota(jnp.int32, (chunk, chunk), 1)
        before = jnp.where((t0 // tok == t1 // tok) & (t0 < t1), 1.0, 0.0).astype(BF)
        r0 = lax.broadcasted_iota(jnp.int32, (rows, chunk), 0)
        r1 = lax.broadcasted_iota(jnp.int32, (rows, chunk), 1)
        same = r0 // cap == r1 // tok
        slot = (r0 % cap).astype(F32)
        for j in range(2):
            expert = (2 * e + j).astype(F32)
            named = jnp.sum(jnp.where(flat[0:8] == expert, 1.0, 0.0), axis=0, keepdims=True)
            named = jnp.broadcast_to(named, (16, chunk))
            rank = jnp.dot(named.astype(BF), before, preferred_element_type=F32)
            hit = same & (slot == rank[0:1]) & (named[0:1] > 0.5)
            pick[q, j * rows : (j + 1) * rows, :] = jnp.where(hit, 1.0, 0.0).astype(BF)
        for n in list(range(0, piece, STEP)) + [piece]:
            at = slice(n, min(n + STEP, piece + LANES))
            value = jnp.dot(pick[q], grid[q, :, at], preferred_element_type=F32).astype(BF)
            for j in range(2):
                packed[j, at_place(q), at] = value[j * rows : (j + 1) * rows]

    values = {}

    def span(group):
        first = ORDER.index(group[0]) * rows
        return slice(first, first + len(group) * rows)

    def up(*group):
        for q in group:
            compact(q)
        here = span(group)
        for j in range(2):
            if group[0] == 0:
                if j == 0:
                    loads[4].wait()
                    loads[5].wait()
                loads[6 + j].wait()
            low = lax.dot_general(
                packed[j, here, 0:piece],
                a_in[j],
                (((1,), (1,)), ((), ())),
                preferred_element_type=F32,
            )
            tenant = packed[j, here, piece + 24 : piece + 25].astype(F32)
            owner = (lax.broadcasted_iota(jnp.int32, low.shape, 1) // RANK).astype(F32)
            low = jnp.where(owner == tenant, low, 0.0).astype(BF)
            for n in range(0, units, STEP):
                at = slice(n, n + STEP)
                value = jnp.dot(
                    packed[j, here, 0:piece], w_up[j, :, at], preferred_element_type=F32
                )
                value = value + jnp.dot(low, a_out[j, :, at], preferred_element_type=F32)
                part[j, here, at] = value.astype(BF)
            for q in group:
                spot = at_place(q)
                values[q, j] = go(
                    part.at[j, spot], peer.at[j, spot], v_s.at[q, j], v_r.at[q, j], x_dev
                )

    cores, rights, lines = {}, {}, {}
    wide = piece // 2

    def down(*group):
        here = span(group)
        gates_of = []
        for j in range(2):
            for q in group:
                values[q, j].wait_recv()
            info = packed[j, here, piece:].astype(F32)
            expert = (2 * e + j).astype(F32)
            gate = jnp.where(info[:, 0:8] == expert, info[:, 8:16] + info[:, 16:24], 0.0)
            gates_of.append(jnp.sum(gate, axis=1, keepdims=True))
            value = part[j, here].astype(F32) + peer[j, here].astype(F32)
            active[j, 0 : len(group) * rows] = (value / (1.0 + jnp.exp(-value))).astype(BF)
        backs = [
            lax.dot_general(
                equal_iota((chunk, chunk)).astype(BF),
                pick[q],
                (((1,), (1,)), ((), ())),
                preferred_element_type=F32,
            ).astype(BF)
            for q in group
        ]
        for h in range(2):
            for n in range(0, wide, STEP):
                full = slice(h * wide + n, h * wide + n + STEP)
                for j in range(2):
                    value = jnp.dot(
                        active[j, 0 : len(group) * rows],
                        w_down[j, :, full],
                        preferred_element_type=F32,
                    )
                    value = (value * gates_of[j]).astype(BF)
                    for n_at, q in enumerate(group):
                        rows_out[q, j * rows : (j + 1) * rows, full] = value[
                            n_at * rows : (n_at + 1) * rows
                        ]
            for q, back in zip(group, backs):
                for n in range(0, wide, STEP):
                    full = slice(h * wide + n, h * wide + n + STEP)
                    y_part[q, h, :, n : n + STEP] = jnp.dot(
                        back, rows_out[q, :, full], preferred_element_type=F32
                    ).astype(BF)
                for r in (1, 0):
                    cores[q, h, r] = go(
                        y_part.at[q, h, lane(r, 1 - c)],
                        core_in.at[q, h, r],
                        c_s.at[q, h, r],
                        c_r.at[q, h, r],
                        c_dev,
                    )

    def add_core(q):
        for h in range(2):
            cores[q, h, 1].wait_recv()
            y_send[q, h] = (
                y_part[q, h, lane(1, c)].astype(F32) + core_in[q, h, 1].astype(F32)
            ).astype(BF)
            rights[q, h] = go(
                y_send.at[q, h], y_in.at[q, h], y_s.at[q, h], y_r.at[q, h], y_dev
            )

    def add_y(q):
        for h in range(2):
            cores[q, h, 0].wait_recv()
            rights[q, h].wait_recv()
            value = (
                y_part[q, h, lane(0, c)].astype(F32)
                + core_in[q, h, 0].astype(F32)
                + y_in[q, h].astype(F32)
            )
            if q == 2:
                lines[3, h].wait_recv()
                value = value + z_in[3, h].astype(F32)
            z_send[q, h] = value.astype(BF)
            if q:
                lines[q, h] = go(
                    z_send.at[q, h],
                    z_in.at[q, h],
                    z_s.at[q, h],
                    z_r.at[q, h],
                    z_dev[2 if q == 2 else 1],
                )

    remote(first_out, grid.at[0, half(1 - x)], tx_s, tx_r, x_dev).wait_recv()
    send_c(0, 0)
    send_y(0)
    send_z(2, 2)
    send_z(1, 1)
    wait_y(0)
    up(0)
    wait_z(2)
    wait_z(1)
    wait_y(2)
    up(2)
    wait_z(3)
    wait_y(1)
    wait_y(3)
    up(3)
    up(1)
    loads[8].wait()
    loads[9].wait()
    down(0, 2)
    add_core(2)
    add_core(0)
    add_y(0)
    down(3)
    add_core(3)
    add_y(3)
    down(1)
    add_core(1)
    add_y(2)
    add_y(1)
    lasts = []
    for h in range(2):
        total = z_send[0, h].astype(F32)
        for q in (2, 1):
            lines[q, h].wait_recv()
            total = total + z_in[q, h].astype(F32)
        x_send[h] = total.astype(BF).reshape(2, tok, wide)
        lasts.append(go(x_send.at[h, 1 - x], x_in.at[h], x_s.at[h], x_r.at[h], x_dev))
        out[:, pl.ds(pl.multiple_of(x * piece + h * wide, wide), wide)] = x_send[h, x]
    for h in range(2):
        lasts[h].wait_recv()
        out[:, pl.ds(pl.multiple_of((1 - x) * piece + h * wide, wide), wide)] = x_in[h]
    for cp in sends:
        cp.wait_send()


def fused(
    tokens, route_ids, gate_weights, tenant_ids, up_weight, down_weight, adapter_in, adapter_out
):
    tok = tokens.shape[0]
    piece = up_weight.shape[1]
    units = up_weight.shape[2]
    cols = adapter_in.shape[2]
    experts_all = up_weight.shape[0] * lax.axis_size("expert")
    cap = max(2, 2 * tok * route_ids.shape[1] // experts_all)
    a_in_t = jnp.swapaxes(adapter_in, 1, 2)
    unit = 2 * tok
    size = 2 * unit
    chunk = 2 * size
    rows = (chunk // tok) * cap
    dma = pltpu.SemaphoreType.DMA
    vm = lambda *shape: pltpu.VMEM(shape, BF)
    any_spec = pl.BlockSpec(memory_space=pl.ANY)
    vmem_spec = pl.BlockSpec(memory_space=pltpu.VMEM)
    return pl.pallas_call(
        functools.partial(expert_kernel, (tok, cap, piece, units, cols)),
        out_shape=jax.ShapeDtypeStruct(tokens.shape, BF),
        in_specs=[any_spec] * 8,
        out_specs=vmem_spec,
        scratch_shapes=[
            vm(*tokens.shape),
            pltpu.VMEM(route_ids.shape[::-1], jnp.int32),
            pltpu.VMEM(gate_weights.shape[::-1], F32),
            pltpu.VMEM((1, tok), jnp.int32),
            vm(*up_weight.shape),
            vm(*down_weight.shape),
            vm(*a_in_t.shape),
            vm(*adapter_out.shape),
            vm(tok, piece + LANES),
            vm(NZ, chunk, piece + LANES),
            vm(2, NZ * rows, piece + LANES),
            vm(NZ, 2 * rows, chunk),
            vm(2, NZ * rows, units),
            vm(2, NZ * rows, units),
            vm(2, 2 * rows, units),
            vm(NZ, 2 * rows, piece),
            vm(NZ, 2, chunk, piece // 2),
            vm(NZ, 2, 2, unit, piece // 2),
            vm(NZ, 2, unit, piece // 2),
            vm(NZ, 2, unit, piece // 2),
            vm(NZ, 2, unit, piece // 2),
            vm(NZ, 2, unit, piece // 2),
            vm(2, 2, tok, piece // 2),
            vm(2, tok, piece // 2),
            dma((10,)),
            dma,
            dma,
            dma((NZ,)),
            dma((NZ,)),
            dma((NZ,)),
            dma((NZ,)),
            dma((NZ, 2)),
            dma((NZ, 2)),
            dma((NZ, 2)),
            dma((NZ, 2)),
            dma((NZ, 2, 2)),
            dma((NZ, 2, 2)),
            dma((NZ, 2)),
            dma((NZ, 2)),
            dma((NZ, 2)),
            dma((NZ, 2)),
            dma((2,)),
            dma((2,)),
        ],
        compiler_params=pltpu.CompilerParams(
            collective_id=0, has_side_effects=True, vmem_limit_bytes=60 * 1024 * 1024
        ),
    )(
        tokens,
        route_ids.T,
        gate_weights.T,
        tenant_ids.reshape(1, tok),
        up_weight,
        down_weight,
        a_in_t,
        adapter_out,
    )


def per_device(
    tokens, route_ids, gate_weights, tenant_ids, up_weight, down_weight, adapter_in, adapter_out
):
    n_dp = lax.axis_size("dp")
    n_col = lax.axis_size("expert")
    tok_count = tokens.shape[0]
    chosen = route_ids.shape[1]
    features = tokens.shape[1]
    exp_local = up_weight.shape[0]
    piece = up_weight.shape[1]
    units = up_weight.shape[2]
    adapter_cols = adapter_in.shape[2]
    experts_all = exp_local * n_col
    capacity = max(2, 2 * tok_count * chosen // experts_all)
    send_rows = experts_all * capacity
    flat_routes = route_ids.reshape(-1)
    order = jnp.arange(flat_routes.shape[0], dtype=jnp.int32)
    same = flat_routes[:, None] == flat_routes[None, :]
    earlier = order[None, :] < order[:, None]
    rank = jnp.sum((same & earlier).astype(jnp.int32), axis=1)
    target = flat_routes * capacity + rank
    outgoing = (
        jnp.zeros((send_rows, features), jnp.bfloat16)
        .at[target]
        .set(jnp.repeat(tokens, chosen, axis=0))
    )
    tag_line = (
        jnp.full((send_rows,), -1.0, jnp.float32)
        .at[target]
        .set(jnp.repeat(tenant_ids, chosen).astype(jnp.float32))
    )
    tag_grid = jnp.broadcast_to(tag_line[:, None], (send_rows, n_dp)).astype(jnp.bfloat16)
    sending = outgoing.reshape(n_col, exp_local, capacity, n_dp, piece)
    tag_send = tag_grid.reshape(n_col, exp_local, capacity, n_dp, 1)
    arrived, arrived_tags = (
        lax.all_to_all(
            lax.all_to_all(sending, "dp", split_axis=3, concat_axis=2, tiled=True),
            "expert",
            split_axis=0,
            concat_axis=2,
            tiled=True,
        ),
        lax.all_to_all(
            lax.all_to_all(tag_send, "dp", split_axis=3, concat_axis=2, tiled=True),
            "expert",
            split_axis=0,
            concat_axis=2,
            tiled=True,
        ),
    )
    rows_all = arrived.shape[2]
    grid = arrived.reshape(exp_local, rows_all, piece)
    tags = arrived_tags.reshape(exp_local, rows_all).astype(jnp.float32)
    up_part = jnp.einsum("erd,edf->erf", grid, up_weight, preferred_element_type=jnp.float32)
    shrink_part = jnp.einsum("erd,edl->erl", grid, adapter_in, preferred_element_type=jnp.float32)
    owner = (jnp.arange(adapter_cols, dtype=jnp.int32) // RANK).astype(jnp.float32)
    shrink = lax.psum(shrink_part.astype(jnp.bfloat16), "dp").astype(jnp.float32)
    keep = owner[None, None, :] == tags[..., None]
    masked_values = jnp.where(keep, shrink, jnp.zeros((), jnp.float32))
    up_portion = lax.psum_scatter(
        up_part.astype(jnp.bfloat16), "dp", scatter_dimension=2, tiled=True
    ).astype(jnp.float32)
    share = units // n_dp
    mapping_portion = lax.dynamic_slice_in_dim(
        adapter_out, lax.axis_index("dp") * share, share, 2
    ).astype(jnp.float32)
    low_rank_adapter = jnp.einsum(
        "erl,elf->erf", masked_values, mapping_portion, precision=lax.Precision.HIGHEST
    )
    hidden_portion = jax.nn.silu(up_portion + low_rank_adapter).astype(jnp.bfloat16)
    hidden_activations = lax.all_gather(hidden_portion, "dp", axis=2, tiled=True)
    expert_out = jnp.einsum(
        "erf,efd->erd", hidden_activations, down_weight, preferred_element_type=jnp.float32
    ).astype(jnp.bfloat16)
    going_back = expert_out.reshape(1, exp_local, rows_all, 1, piece)
    returned = lax.all_to_all(
        lax.all_to_all(going_back, "expert", split_axis=2, concat_axis=0, tiled=True),
        "dp",
        split_axis=2,
        concat_axis=3,
        tiled=True,
    )
    results = returned.reshape(send_rows, features)
    picked = results[target].astype(jnp.float32).reshape(tok_count, chosen, features)
    mixed = jnp.sum(picked * gate_weights[:, :, None], axis=1)
    return mixed.astype(jnp.bfloat16)


def solution(mesh):
    placed = (
        P(("dp", "expert"), None),
        P(("dp", "expert"), None),
        P(("dp", "expert"), None),
        P(("dp", "expert")),
        P("expert", "dp", None),
        P("expert", None, "dp"),
        P("expert", "dp", None),
        P("expert", None, None),
    )
    small = mesh.shape["dp"] == 2 and mesh.shape["expert"] == 4 * NZ
    return jax.shard_map(
        fused if small else per_device, mesh=mesh, in_specs=placed, out_specs=P(("dp", "expert"), None), check_vma=False
    )
```

```python
import functools

import jax
import jax.numpy as jnp
from jax import lax
from jax.experimental import pallas as pl
from jax.experimental.pallas import tpu as pltpu
from jax.sharding import PartitionSpec as P

RANK = 16
MESH = pl.DeviceIdType.MESH
BF = jnp.bfloat16
F32 = jnp.float32
LANES = 128
NZ = 4
STEP = 256
ORDER = (0, 2, 3, 1)


def equal_iota(shape):
    same = lax.broadcasted_iota(jnp.int32, shape, 0) == lax.broadcasted_iota(jnp.int32, shape, 1)
    return jnp.where(same, 1.0, 0.0)


def expert_kernel(
    dims,
    tokens_hbm,
    routes_hbm,
    gates_hbm,
    tenants_hbm,
    w_up_hbm,
    w_down_hbm,
    a_in_hbm,
    a_out_hbm,
    out,
    tokens,
    routes_t,
    gates_t,
    tenants_t,
    w_up,
    w_down,
    a_in,
    a_out,
    first_out,
    grid,
    packed,
    pick,
    part,
    peer,
    rows_out,
    y_part,
    core_in,
    y_send,
    y_in,
    z_send,
    z_in,
    x_send,
    x_in,
    load_sem,
    tx_s,
    tx_r,
    ty_s,
    ty_r,
    tz_s,
    tz_r,
    tc_s,
    tc_r,
    v_s,
    v_r,
    c_s,
    c_r,
    y_s,
    y_r,
    z_s,
    z_r,
    x_s,
    x_r,
):
    tok, cap, piece, units, cols = dims
    unit = 2 * tok
    size = 2 * unit
    chunk = 2 * size
    rows = (chunk // tok) * cap
    x = lax.axis_index("dp")
    e = lax.axis_index("expert")
    z = e // 4
    y = (e // 2) % 2
    c = e % 2
    x_dev = (1 - x, e)
    y_dev = (x, z * 4 + (1 - y) * 2 + c)
    c_dev = (x, z * 4 + y * 2 + (1 - c))
    z_of = {1: z + 1 - 2 * (z % 2), 2: (z + 2) % 4}
    z_dev = {q: (x, z_of[q] * 4 + y * 2 + c) for q in z_of}

    def remote(src, dst, ss, rs, dev):
        return pltpu.make_async_remote_copy(
            src_ref=src, dst_ref=dst, send_sem=ss, recv_sem=rs, device_id=dev, device_id_type=MESH
        )

    pairs = [
        (tokens_hbm, tokens),
        (routes_hbm, routes_t),
        (gates_hbm, gates_t),
        (tenants_hbm, tenants_t),
        (a_in_hbm, a_in),
        (a_out_hbm, a_out),
        (w_up_hbm.at[0], w_up.at[0]),
        (w_up_hbm.at[1], w_up.at[1]),
        (w_down_hbm.at[0], w_down.at[0]),
        (w_down_hbm.at[1], w_down.at[1]),
    ]
    loads = [
        pltpu.make_async_copy(src, dst, load_sem.at[n]) for n, (src, dst) in enumerate(pairs)
    ]
    for copy in loads:
        copy.start()

    barrier = pltpu.get_barrier_semaphore()
    for dev in [x_dev, y_dev, c_dev] + [z_dev[q] for q in z_of]:
        pl.semaphore_signal(barrier, inc=1, device_id=dev, device_id_type=MESH)

    for n in range(4):
        loads[n].wait()
    gates = gates_t[...]
    high = gates.astype(BF).astype(F32)
    stacked = jnp.concatenate(
        [
            routes_t[...].astype(F32),
            high,
            gates - high,
            jnp.broadcast_to(tenants_t[...].astype(F32), (8, tok)),
        ],
        axis=0,
    )
    meta = lax.dot_general(
        stacked, equal_iota((32, LANES)), (((0,), (0,)), ((), ())), preferred_element_type=F32
    ).astype(BF)

    def lane(r, core):
        return pl.ds(pl.multiple_of(r * size + core * unit, unit), unit)

    def half(dp):
        return pl.ds(pl.multiple_of(c * unit + dp * tok, tok), tok)

    first_out[:, 0:piece] = tokens[:, pl.ds(pl.multiple_of((1 - x) * piece, piece), piece)]
    first_out[:, piece:] = meta
    grid[0, half(x), 0:piece] = tokens[:, pl.ds(pl.multiple_of(x * piece, piece), piece)]
    grid[0, half(x), piece:] = meta
    pl.semaphore_wait(barrier, 5)

    sends = []

    def go(*args):
        cp = remote(*args)
        cp.start()
        sends.append(cp)
        return cp

    go(first_out, grid.at[0, half(x)], tx_s, tx_r, x_dev)

    def send_y(q):
        go(grid.at[q, lane(0, c)], grid.at[q, lane(1, c)], ty_s.at[q], ty_r.at[q], y_dev)

    def wait_y(q):
        here = grid.at[q, lane(1, c)]
        remote(here, here, ty_s.at[q], ty_r.at[q], y_dev).wait_recv()
        send_c(q, 1)

    def send_z(q, dev):
        src = grid.at[2 if q == 3 else 0, lane(0, c)]
        go(src, grid.at[q, lane(0, c)], tz_s.at[q], tz_r.at[q], z_dev[dev])

    def wait_z(q):
        here = grid.at[q, lane(0, c)]
        remote(here, here, tz_s.at[q], tz_r.at[q], z_dev[q % 2 or 2]).wait_recv()
        if q == 2:
            send_z(3, 1)
        send_c(q, 0)
        send_y(q)

    def send_c(q, r):
        here = grid.at[q, lane(r, c)]
        go(here, here, tc_s.at[q, r], tc_r.at[q, r], c_dev)

    def at_place(q):
        first = ORDER.index(q) * rows
        return slice(first, first + rows)

    def compact(q):
        for r in range(2):
            here = grid.at[q, lane(r, 1 - c)]
            remote(here, here, tc_s.at[q, r], tc_r.at[q, r], c_dev).wait_recv()
        flat = lax.dot_general(
            equal_iota((LANES, LANES)).astype(BF),
            grid[q, :, piece:],
            (((1,), (1,)), ((), ())),
            preferred_element_type=F32,
        )
        t0 = lax.broadcasted_iota(jnp.int32, (chunk, chunk), 0)
        t1 = lax.broadcasted_iota(jnp.int32, (chunk, chunk), 1)
        before = jnp.where((t0 // tok == t1 // tok) & (t0 < t1), 1.0, 0.0).astype(BF)
        r0 = lax.broadcasted_iota(jnp.int32, (rows, chunk), 0)
        r1 = lax.broadcasted_iota(jnp.int32, (rows, chunk), 1)
        same = r0 // cap == r1 // tok
        slot = (r0 % cap).astype(F32)
        for j in range(2):
            expert = (2 * e + j).astype(F32)
            named = jnp.sum(jnp.where(flat[0:8] == expert, 1.0, 0.0), axis=0, keepdims=True)
            named = jnp.broadcast_to(named, (16, chunk))
            rank = jnp.dot(named.astype(BF), before, preferred_element_type=F32)
            hit = same & (slot == rank[0:1]) & (named[0:1] > 0.5)
            pick[q, j * rows : (j + 1) * rows, :] = jnp.where(hit, 1.0, 0.0).astype(BF)
        for n in list(range(0, piece, STEP)) + [piece]:
            at = slice(n, min(n + STEP, piece + LANES))
            value = jnp.dot(pick[q], grid[q, :, at], preferred_element_type=F32).astype(BF)
            for j in range(2):
                packed[j, at_place(q), at] = value[j * rows : (j + 1) * rows]

    values = {}

    def span(group):
        first = ORDER.index(group[0]) * rows
        return slice(first, first + len(group) * rows)

    def send_v(q, j):
        spot = at_place(q)
        values[q, j] = go(part.at[j, spot], peer.at[j, spot], v_s.at[q, j], v_r.at[q, j], x_dev)

    def up(*group):
        for q in group:
            compact(q)
        here = span(group)
        for j in range(2):
            if group[0] == 0:
                if j == 0:
                    loads[4].wait()
                    loads[5].wait()
                loads[6 + j].wait()
            low = lax.dot_general(
                packed[j, here, 0:piece],
                a_in[j],
                (((1,), (1,)), ((), ())),
                preferred_element_type=F32,
            )
            tenant = packed[j, here, piece + 24 : piece + 25].astype(F32)
            owner = (lax.broadcasted_iota(jnp.int32, low.shape, 1) // RANK).astype(F32)
            low = jnp.where(owner == tenant, low, 0.0).astype(BF)
            for n in range(0, units, STEP):
                at = slice(n, n + STEP)
                value = jnp.dot(
                    packed[j, here, 0:piece], w_up[j, :, at], preferred_element_type=F32
                )
                value = value + jnp.dot(low, a_out[j, :, at], preferred_element_type=F32)
                part[j, here, at] = value.astype(BF)
            send_v(group[0], j)
        for q in group[1:]:
            for j in range(2):
                send_v(q, j)

    cores, rights, lines = {}, {}, {}
    wide = piece // 2

    def down(*group):
        here = span(group)
        for j in range(2):
            for q in group:
                values[q, j].wait_recv()
            info = packed[j, here, piece:].astype(F32)
            expert = (2 * e + j).astype(F32)
            gate = jnp.where(info[:, 0:8] == expert, info[:, 8:16] + info[:, 16:24], 0.0)
            gate = jnp.sum(gate, axis=1, keepdims=True)
            value = part[j, here].astype(F32) + peer[j, here].astype(F32)
            hidden = (value / (1.0 + jnp.exp(-value))).astype(BF)
            for n in range(0, piece, STEP):
                at = slice(n, n + STEP)
                value = jnp.dot(hidden, w_down[j, :, at], preferred_element_type=F32)
                value = (value * gate).astype(BF)
                for n_at, q in enumerate(group):
                    rows_out[q, j * rows : (j + 1) * rows, at] = value[
                        n_at * rows : (n_at + 1) * rows
                    ]
        backs = [
            lax.dot_general(
                equal_iota((chunk, chunk)).astype(BF),
                pick[q],
                (((1,), (1,)), ((), ())),
                preferred_element_type=F32,
            ).astype(BF)
            for q in group
        ]
        for h in range(2):
            for q, back in zip(group, backs):
                for n in range(0, wide, STEP):
                    full = slice(h * wide + n, h * wide + n + STEP)
                    y_part[q, h, :, n : n + STEP] = jnp.dot(
                        back, rows_out[q, :, full], preferred_element_type=F32
                    ).astype(BF)
                for r in (1, 0):
                    cores[q, h, r] = go(
                        y_part.at[q, h, lane(r, 1 - c)],
                        core_in.at[q, h, r],
                        c_s.at[q, h, r],
                        c_r.at[q, h, r],
                        c_dev,
                    )

    def add_core(q):
        for h in range(2):
            cores[q, h, 1].wait_recv()
            y_send[q, h] = (
                y_part[q, h, lane(1, c)].astype(F32) + core_in[q, h, 1].astype(F32)
            ).astype(BF)
            rights[q, h] = go(
                y_send.at[q, h], y_in.at[q, h], y_s.at[q, h], y_r.at[q, h], y_dev
            )

    def add_y(q):
        for h in range(2):
            cores[q, h, 0].wait_recv()
            rights[q, h].wait_recv()
            value = (
                y_part[q, h, lane(0, c)].astype(F32)
                + core_in[q, h, 0].astype(F32)
                + y_in[q, h].astype(F32)
            )
            if q == 2:
                lines[3, h].wait_recv()
                value = value + z_in[3, h].astype(F32)
            z_send[q, h] = value.astype(BF)
            if q:
                lines[q, h] = go(
                    z_send.at[q, h],
                    z_in.at[q, h],
                    z_s.at[q, h],
                    z_r.at[q, h],
                    z_dev[2 if q == 2 else 1],
                )

    remote(first_out, grid.at[0, half(1 - x)], tx_s, tx_r, x_dev).wait_recv()
    send_c(0, 0)
    send_y(0)
    send_z(2, 2)
    send_z(1, 1)
    wait_y(0)
    up(0)
    wait_z(2)
    wait_z(1)
    wait_y(2)
    up(2)
    wait_z(3)
    wait_y(1)
    wait_y(3)
    up(3, 1)
    loads[8].wait()
    loads[9].wait()
    down(0, 2)
    add_core(2)
    add_core(0)
    down(3)
    add_core(3)
    add_y(0)
    down(1)
    add_core(1)
    add_y(3)
    add_y(2)
    add_y(1)
    lasts = []
    for h in range(2):
        total = z_send[0, h].astype(F32)
        for q in (2, 1):
            lines[q, h].wait_recv()
            total = total + z_in[q, h].astype(F32)
        x_send[h] = total.astype(BF).reshape(2, tok, wide)
        lasts.append(go(x_send.at[h, 1 - x], x_in.at[h], x_s.at[h], x_r.at[h], x_dev))
        out[:, pl.ds(pl.multiple_of(x * piece + h * wide, wide), wide)] = x_send[h, x]
    for h in range(2):
        lasts[h].wait_recv()
        out[:, pl.ds(pl.multiple_of((1 - x) * piece + h * wide, wide), wide)] = x_in[h]
    for cp in sends:
        cp.wait_send()


def fused(
    tokens, route_ids, gate_weights, tenant_ids, up_weight, down_weight, adapter_in, adapter_out
):
    tok = tokens.shape[0]
    piece = up_weight.shape[1]
    units = up_weight.shape[2]
    cols = adapter_in.shape[2]
    experts_all = up_weight.shape[0] * lax.axis_size("expert")
    cap = max(2, 2 * tok * route_ids.shape[1] // experts_all)
    a_in_t = jnp.swapaxes(adapter_in, 1, 2)
    unit = 2 * tok
    size = 2 * unit
    chunk = 2 * size
    rows = (chunk // tok) * cap
    dma = pltpu.SemaphoreType.DMA
    vm = lambda *shape: pltpu.VMEM(shape, BF)
    any_spec = pl.BlockSpec(memory_space=pl.ANY)
    vmem_spec = pl.BlockSpec(memory_space=pltpu.VMEM)
    return pl.pallas_call(
        functools.partial(expert_kernel, (tok, cap, piece, units, cols)),
        out_shape=jax.ShapeDtypeStruct(tokens.shape, BF),
        in_specs=[any_spec] * 8,
        out_specs=vmem_spec,
        scratch_shapes=[
            vm(*tokens.shape),
            pltpu.VMEM(route_ids.shape[::-1], jnp.int32),
            pltpu.VMEM(gate_weights.shape[::-1], F32),
            pltpu.VMEM((1, tok), jnp.int32),
            vm(*up_weight.shape),
            vm(*down_weight.shape),
            vm(*a_in_t.shape),
            vm(*adapter_out.shape),
            vm(tok, piece + LANES),
            vm(NZ, chunk, piece + LANES),
            vm(2, NZ * rows, piece + LANES),
            vm(NZ, 2 * rows, chunk),
            vm(2, NZ * rows, units),
            vm(2, NZ * rows, units),
            vm(NZ, 2 * rows, piece),
            vm(NZ, 2, chunk, piece // 2),
            vm(NZ, 2, 2, unit, piece // 2),
            vm(NZ, 2, unit, piece // 2),
            vm(NZ, 2, unit, piece // 2),
            vm(NZ, 2, unit, piece // 2),
            vm(NZ, 2, unit, piece // 2),
            vm(2, 2, tok, piece // 2),
            vm(2, tok, piece // 2),
            dma((10,)),
            dma,
            dma,
            dma((NZ,)),
            dma((NZ,)),
            dma((NZ,)),
            dma((NZ,)),
            dma((NZ, 2)),
            dma((NZ, 2)),
            dma((NZ, 2)),
            dma((NZ, 2)),
            dma((NZ, 2, 2)),
            dma((NZ, 2, 2)),
            dma((NZ, 2)),
            dma((NZ, 2)),
            dma((NZ, 2)),
            dma((NZ, 2)),
            dma((2,)),
            dma((2,)),
        ],
        compiler_params=pltpu.CompilerParams(
            collective_id=0, has_side_effects=True, vmem_limit_bytes=60 * 1024 * 1024
        ),
    )(
        tokens,
        route_ids.T,
        gate_weights.T,
        tenant_ids.reshape(1, tok),
        up_weight,
        down_weight,
        a_in_t,
        adapter_out,
    )


def per_device(
    tokens, route_ids, gate_weights, tenant_ids, up_weight, down_weight, adapter_in, adapter_out
):
    n_dp = lax.axis_size("dp")
    n_col = lax.axis_size("expert")
    tok_count = tokens.shape[0]
    chosen = route_ids.shape[1]
    features = tokens.shape[1]
    exp_local = up_weight.shape[0]
    piece = up_weight.shape[1]
    units = up_weight.shape[2]
    adapter_cols = adapter_in.shape[2]
    experts_all = exp_local * n_col
    capacity = max(2, 2 * tok_count * chosen // experts_all)
    send_rows = experts_all * capacity
    flat_routes = route_ids.reshape(-1)
    order = jnp.arange(flat_routes.shape[0], dtype=jnp.int32)
    same = flat_routes[:, None] == flat_routes[None, :]
    earlier = order[None, :] < order[:, None]
    rank = jnp.sum((same & earlier).astype(jnp.int32), axis=1)
    target = flat_routes * capacity + rank
    outgoing = (
        jnp.zeros((send_rows, features), jnp.bfloat16)
        .at[target]
        .set(jnp.repeat(tokens, chosen, axis=0))
    )
    tag_line = (
        jnp.full((send_rows,), -1.0, jnp.float32)
        .at[target]
        .set(jnp.repeat(tenant_ids, chosen).astype(jnp.float32))
    )
    tag_grid = jnp.broadcast_to(tag_line[:, None], (send_rows, n_dp)).astype(jnp.bfloat16)
    sending = outgoing.reshape(n_col, exp_local, capacity, n_dp, piece)
    tag_send = tag_grid.reshape(n_col, exp_local, capacity, n_dp, 1)
    arrived, arrived_tags = (
        lax.all_to_all(
            lax.all_to_all(sending, "dp", split_axis=3, concat_axis=2, tiled=True),
            "expert",
            split_axis=0,
            concat_axis=2,
            tiled=True,
        ),
        lax.all_to_all(
            lax.all_to_all(tag_send, "dp", split_axis=3, concat_axis=2, tiled=True),
            "expert",
            split_axis=0,
            concat_axis=2,
            tiled=True,
        ),
    )
    rows_all = arrived.shape[2]
    grid = arrived.reshape(exp_local, rows_all, piece)
    tags = arrived_tags.reshape(exp_local, rows_all).astype(jnp.float32)
    up_part = jnp.einsum("erd,edf->erf", grid, up_weight, preferred_element_type=jnp.float32)
    shrink_part = jnp.einsum("erd,edl->erl", grid, adapter_in, preferred_element_type=jnp.float32)
    owner = (jnp.arange(adapter_cols, dtype=jnp.int32) // RANK).astype(jnp.float32)
    shrink = lax.psum(shrink_part.astype(jnp.bfloat16), "dp").astype(jnp.float32)
    keep = owner[None, None, :] == tags[..., None]
    masked_values = jnp.where(keep, shrink, jnp.zeros((), jnp.float32))
    up_portion = lax.psum_scatter(
        up_part.astype(jnp.bfloat16), "dp", scatter_dimension=2, tiled=True
    ).astype(jnp.float32)
    share = units // n_dp
    mapping_portion = lax.dynamic_slice_in_dim(
        adapter_out, lax.axis_index("dp") * share, share, 2
    ).astype(jnp.float32)
    low_rank_adapter = jnp.einsum(
        "erl,elf->erf", masked_values, mapping_portion, precision=lax.Precision.HIGHEST
    )
    hidden_portion = jax.nn.silu(up_portion + low_rank_adapter).astype(jnp.bfloat16)
    hidden_activations = lax.all_gather(hidden_portion, "dp", axis=2, tiled=True)
    expert_out = jnp.einsum(
        "erf,efd->erd", hidden_activations, down_weight, preferred_element_type=jnp.float32
    ).astype(jnp.bfloat16)
    going_back = expert_out.reshape(1, exp_local, rows_all, 1, piece)
    returned = lax.all_to_all(
        lax.all_to_all(going_back, "expert", split_axis=2, concat_axis=0, tiled=True),
        "dp",
        split_axis=2,
        concat_axis=3,
        tiled=True,
    )
    results = returned.reshape(send_rows, features)
    picked = results[target].astype(jnp.float32).reshape(tok_count, chosen, features)
    mixed = jnp.sum(picked * gate_weights[:, :, None], axis=1)
    return mixed.astype(jnp.bfloat16)


def solution(mesh):
    placed = (
        P(("dp", "expert"), None),
        P(("dp", "expert"), None),
        P(("dp", "expert"), None),
        P(("dp", "expert")),
        P("expert", "dp", None),
        P("expert", None, "dp"),
        P("expert", "dp", None),
        P("expert", None, None),
    )
    small = mesh.shape["dp"] == 2 and mesh.shape["expert"] == 4 * NZ
    return jax.shard_map(
        fused if small else per_device, mesh=mesh, in_specs=placed, out_specs=P(("dp", "expert"), None), check_vma=False
    )
```

```python
import functools

import jax
import jax.numpy as jnp
from jax import lax
from jax.experimental import pallas as pl
from jax.experimental.pallas import tpu as pltpu
from jax.sharding import PartitionSpec as P

RANK = 16
MESH = pl.DeviceIdType.MESH
BF = jnp.bfloat16
F32 = jnp.float32
LANES = 128
NZ = 4
STEP = 256
ORDER = (0, 2, 3, 1)


def equal_iota(shape):
    same = lax.broadcasted_iota(jnp.int32, shape, 0) == lax.broadcasted_iota(jnp.int32, shape, 1)
    return jnp.where(same, 1.0, 0.0)


def expert_kernel(
    dims,
    tokens_hbm,
    routes_hbm,
    gates_hbm,
    tenants_hbm,
    w_up_hbm,
    w_down_hbm,
    a_in_hbm,
    a_out_hbm,
    out,
    tokens,
    routes_t,
    gates_t,
    tenants_t,
    w_up,
    w_down,
    a_in,
    a_out,
    first_out,
    grid,
    packed,
    pick,
    part,
    peer,
    rows_out,
    y_part,
    core_in,
    y_send,
    y_in,
    z_send,
    z_in,
    x_send,
    x_in,
    load_sem,
    tx_s,
    tx_r,
    ty_s,
    ty_r,
    tz_s,
    tz_r,
    tc_s,
    tc_r,
    v_s,
    v_r,
    c_s,
    c_r,
    y_s,
    y_r,
    z_s,
    z_r,
    x_s,
    x_r,
):
    tok, cap, piece, units, cols = dims
    unit = 2 * tok
    size = 2 * unit
    chunk = 2 * size
    rows = (chunk // tok) * cap
    x = lax.axis_index("dp")
    e = lax.axis_index("expert")
    z = e // 4
    y = (e // 2) % 2
    c = e % 2
    x_dev = (1 - x, e)
    y_dev = (x, z * 4 + (1 - y) * 2 + c)
    c_dev = (x, z * 4 + y * 2 + (1 - c))
    z_of = {1: z + 1 - 2 * (z % 2), 2: (z + 2) % 4, 3: 3 - z}
    z_dev = {q: (x, z_of[q] * 4 + y * 2 + c) for q in z_of}

    def remote(src, dst, ss, rs, dev):
        return pltpu.make_async_remote_copy(
            src_ref=src, dst_ref=dst, send_sem=ss, recv_sem=rs, device_id=dev, device_id_type=MESH
        )

    pairs = [
        (tokens_hbm, tokens),
        (routes_hbm, routes_t),
        (gates_hbm, gates_t),
        (tenants_hbm, tenants_t),
        (a_in_hbm, a_in),
        (a_out_hbm, a_out),
        (w_up_hbm.at[0], w_up.at[0]),
        (w_up_hbm.at[1], w_up.at[1]),
        (w_down_hbm.at[0], w_down.at[0]),
        (w_down_hbm.at[1], w_down.at[1]),
    ]
    loads = [
        pltpu.make_async_copy(src, dst, load_sem.at[n]) for n, (src, dst) in enumerate(pairs)
    ]
    for copy in loads:
        copy.start()

    barrier = pltpu.get_barrier_semaphore()
    for dev in [x_dev, y_dev, c_dev] + [z_dev[q] for q in z_of]:
        pl.semaphore_signal(barrier, inc=1, device_id=dev, device_id_type=MESH)

    for n in range(4):
        loads[n].wait()
    gates = gates_t[...]
    high = gates.astype(BF).astype(F32)
    stacked = jnp.concatenate(
        [
            routes_t[...].astype(F32),
            high,
            gates - high,
            jnp.broadcast_to(tenants_t[...].astype(F32), (8, tok)),
        ],
        axis=0,
    )
    meta = lax.dot_general(
        stacked, equal_iota((32, LANES)), (((0,), (0,)), ((), ())), preferred_element_type=F32
    ).astype(BF)

    def lane(r, core):
        return pl.ds(pl.multiple_of(r * size + core * unit, unit), unit)

    def half(dp):
        return pl.ds(pl.multiple_of(c * unit + dp * tok, tok), tok)

    first_out[:, 0:piece] = tokens[:, pl.ds(pl.multiple_of((1 - x) * piece, piece), piece)]
    first_out[:, piece:] = meta
    grid[0, half(x), 0:piece] = tokens[:, pl.ds(pl.multiple_of(x * piece, piece), piece)]
    grid[0, half(x), piece:] = meta
    pl.semaphore_wait(barrier, 6)

    sends = []

    def go(*args):
        cp = remote(*args)
        cp.start()
        sends.append(cp)
        return cp

    go(first_out, grid.at[0, half(x)], tx_s, tx_r, x_dev)

    def send_y(q):
        go(grid.at[q, lane(0, c)], grid.at[q, lane(1, c)], ty_s.at[q], ty_r.at[q], y_dev)

    def wait_y(q):
        here = grid.at[q, lane(1, c)]
        remote(here, here, ty_s.at[q], ty_r.at[q], y_dev).wait_recv()
        send_c(q, 1)

    def send_z(q, dev):
        src = grid.at[2 if q == 3 else 0, lane(0, c)]
        go(src, grid.at[q, lane(0, c)], tz_s.at[q], tz_r.at[q], z_dev[dev])

    def wait_z(q):
        here = grid.at[q, lane(0, c)]
        remote(here, here, tz_s.at[q], tz_r.at[q], z_dev[q % 2 or 2]).wait_recv()
        if q == 2:
            send_z(3, 1)
        send_c(q, 0)
        send_y(q)

    def send_c(q, r):
        here = grid.at[q, lane(r, c)]
        go(here, here, tc_s.at[q, r], tc_r.at[q, r], c_dev)

    def at_place(q):
        first = ORDER.index(q) * rows
        return slice(first, first + rows)

    def compact(q):
        for r in range(2):
            here = grid.at[q, lane(r, 1 - c)]
            remote(here, here, tc_s.at[q, r], tc_r.at[q, r], c_dev).wait_recv()
        flat = lax.dot_general(
            equal_iota((LANES, LANES)).astype(BF),
            grid[q, :, piece:],
            (((1,), (1,)), ((), ())),
            preferred_element_type=F32,
        )
        t0 = lax.broadcasted_iota(jnp.int32, (chunk, chunk), 0)
        t1 = lax.broadcasted_iota(jnp.int32, (chunk, chunk), 1)
        before = jnp.where((t0 // tok == t1 // tok) & (t0 < t1), 1.0, 0.0).astype(BF)
        r0 = lax.broadcasted_iota(jnp.int32, (rows, chunk), 0)
        r1 = lax.broadcasted_iota(jnp.int32, (rows, chunk), 1)
        same = r0 // cap == r1 // tok
        slot = (r0 % cap).astype(F32)
        for j in range(2):
            expert = (2 * e + j).astype(F32)
            named = jnp.sum(jnp.where(flat[0:8] == expert, 1.0, 0.0), axis=0, keepdims=True)
            named = jnp.broadcast_to(named, (16, chunk))
            rank = jnp.dot(named.astype(BF), before, preferred_element_type=F32)
            hit = same & (slot == rank[0:1]) & (named[0:1] > 0.5)
            pick[q, j * rows : (j + 1) * rows, :] = jnp.where(hit, 1.0, 0.0).astype(BF)
        for n in list(range(0, piece, STEP)) + [piece]:
            at = slice(n, min(n + STEP, piece + LANES))
            value = jnp.dot(pick[q], grid[q, :, at], preferred_element_type=F32).astype(BF)
            for j in range(2):
                packed[j, at_place(q), at] = value[j * rows : (j + 1) * rows]

    values = {}

    def span(group):
        first = ORDER.index(group[0]) * rows
        return slice(first, first + len(group) * rows)

    def send_v(q, j):
        spot = at_place(q)
        values[q, j] = go(part.at[j, spot], peer.at[j, spot], v_s.at[q, j], v_r.at[q, j], x_dev)

    def up(*group):
        for q in group:
            compact(q)
        here = span(group)
        many = len(group) * rows
        for j in range(2):
            if group[0] == 0:
                if j == 0:
                    loads[4].wait()
                    loads[5].wait()
                loads[6 + j].wait()
            if j == 0:
                low = lax.dot_general(
                    packed[:, here, 0:piece].reshape(2 * many, piece),
                    a_in[...].reshape(2 * cols, piece),
                    (((1,), (1,)), ((), ())),
                    preferred_element_type=F32,
                )
            tenant = packed[j, here, piece + 24 : piece + 25].astype(F32)
            owner = lax.broadcasted_iota(jnp.int32, (many, 2 * cols), 1) // RANK
            owner = (owner - j * (cols // RANK)).astype(F32)
            mine = jnp.where(owner == tenant, low[j * many : (j + 1) * many], 0.0).astype(BF)
            for n in range(0, units, STEP):
                at = slice(n, n + STEP)
                value = jnp.dot(
                    packed[j, here, 0:piece], w_up[j, :, at], preferred_element_type=F32
                )
                value = value + jnp.dot(
                    mine, a_out[:, :, at].reshape(2 * cols, STEP), preferred_element_type=F32
                )
                part[j, here, at] = value.astype(BF)
            send_v(group[0], j)
        for q in group[1:]:
            for j in range(2):
                send_v(q, j)

    cores, rights, lines = {}, {}, {}
    wide = piece // 2

    def down(*group, then=None):
        here = span(group)
        for j in range(2):
            for q in group:
                values[q, j].wait_recv()
            info = packed[j, here, piece:].astype(F32)
            expert = (2 * e + j).astype(F32)
            gate = jnp.where(info[:, 0:8] == expert, info[:, 8:16] + info[:, 16:24], 0.0)
            gate = jnp.sum(gate, axis=1, keepdims=True)
            value = part[j, here].astype(F32) + peer[j, here].astype(F32)
            hidden = (value / (1.0 + jnp.exp(-value))).astype(BF)
            for n in range(0, piece, STEP):
                at = slice(n, n + STEP)
                value = jnp.dot(hidden, w_down[j, :, at], preferred_element_type=F32)
                value = (value * gate).astype(BF)
                for n_at, q in enumerate(group):
                    rows_out[q, j * rows : (j + 1) * rows, at] = value[
                        n_at * rows : (n_at + 1) * rows
                    ]
        if then is not None:
            then()
        backs = [
            lax.dot_general(
                equal_iota((chunk, chunk)).astype(BF),
                pick[q],
                (((1,), (1,)), ((), ())),
                preferred_element_type=F32,
            ).astype(BF)
            for q in group
        ]
        for h in range(2):
            for q, back in zip(group, backs):
                for n in range(0, wide, STEP):
                    full = slice(h * wide + n, h * wide + n + STEP)
                    y_part[q, h, :, n : n + STEP] = jnp.dot(
                        back, rows_out[q, :, full], preferred_element_type=F32
                    ).astype(BF)
                for r in (1, 0):
                    cores[q, h, r] = go(
                        y_part.at[q, h, lane(r, 1 - c)],
                        core_in.at[q, h, r],
                        c_s.at[q, h, r],
                        c_r.at[q, h, r],
                        c_dev,
                    )

    def add_core(q):
        for h in range(2):
            cores[q, h, 1].wait_recv()
            y_send[q, h] = (
                y_part[q, h, lane(1, c)].astype(F32) + core_in[q, h, 1].astype(F32)
            ).astype(BF)
            rights[q, h] = go(
                y_send.at[q, h], y_in.at[q, h], y_s.at[q, h], y_r.at[q, h], y_dev
            )

    def add_y(q):
        for h in range(2):
            cores[q, h, 0].wait_recv()
            rights[q, h].wait_recv()
            value = (
                y_part[q, h, lane(0, c)].astype(F32)
                + core_in[q, h, 0].astype(F32)
                + y_in[q, h].astype(F32)
            )
            z_send[q, h] = value.astype(BF)
            if q:
                lines[q, h] = go(
                    z_send.at[q, h],
                    z_in.at[q, h],
                    z_s.at[q, h],
                    z_r.at[q, h],
                    z_dev[q],
                )

    remote(first_out, grid.at[0, half(1 - x)], tx_s, tx_r, x_dev).wait_recv()
    send_c(0, 0)
    send_y(0)
    send_z(2, 2)
    send_z(1, 1)
    wait_y(0)
    up(0)
    wait_z(2)
    wait_z(1)
    wait_y(2)
    up(2)
    wait_z(3)
    wait_y(1)
    wait_y(3)
    up(3, 1)
    loads[8].wait()
    loads[9].wait()
    down(0, 2)
    add_core(2)
    add_core(0)
    down(3)
    add_core(3)
    add_y(2)
    add_y(0)
    down(1, then=lambda: add_y(3))
    add_core(1)
    add_y(1)
    lasts = []
    for h in range(2):
        total = z_send[0, h].astype(F32)
        for q in (2, 3, 1):
            lines[q, h].wait_recv()
            total = total + z_in[q, h].astype(F32)
        x_send[h] = total.astype(BF).reshape(2, tok, wide)
        lasts.append(go(x_send.at[h, 1 - x], x_in.at[h], x_s.at[h], x_r.at[h], x_dev))
        out[:, pl.ds(pl.multiple_of(x * piece + h * wide, wide), wide)] = x_send[h, x]
    for h in range(2):
        lasts[h].wait_recv()
        out[:, pl.ds(pl.multiple_of((1 - x) * piece + h * wide, wide), wide)] = x_in[h]
    for cp in sends:
        cp.wait_send()


def fused(
    tokens, route_ids, gate_weights, tenant_ids, up_weight, down_weight, adapter_in, adapter_out
):
    tok = tokens.shape[0]
    piece = up_weight.shape[1]
    units = up_weight.shape[2]
    cols = adapter_in.shape[2]
    experts_all = up_weight.shape[0] * lax.axis_size("expert")
    cap = max(2, 2 * tok * route_ids.shape[1] // experts_all)
    a_in_t = jnp.swapaxes(adapter_in, 1, 2)
    unit = 2 * tok
    size = 2 * unit
    chunk = 2 * size
    rows = (chunk // tok) * cap
    dma = pltpu.SemaphoreType.DMA
    vm = lambda *shape: pltpu.VMEM(shape, BF)
    any_spec = pl.BlockSpec(memory_space=pl.ANY)
    vmem_spec = pl.BlockSpec(memory_space=pltpu.VMEM)
    return pl.pallas_call(
        functools.partial(expert_kernel, (tok, cap, piece, units, cols)),
        out_shape=jax.ShapeDtypeStruct(tokens.shape, BF),
        in_specs=[any_spec] * 8,
        out_specs=vmem_spec,
        scratch_shapes=[
            vm(*tokens.shape),
            pltpu.VMEM(route_ids.shape[::-1], jnp.int32),
            pltpu.VMEM(gate_weights.shape[::-1], F32),
            pltpu.VMEM((1, tok), jnp.int32),
            vm(*up_weight.shape),
            vm(*down_weight.shape),
            vm(*a_in_t.shape),
            vm(*adapter_out.shape),
            vm(tok, piece + LANES),
            vm(NZ, chunk, piece + LANES),
            vm(2, NZ * rows, piece + LANES),
            vm(NZ, 2 * rows, chunk),
            vm(2, NZ * rows, units),
            vm(2, NZ * rows, units),
            vm(NZ, 2 * rows, piece),
            vm(NZ, 2, chunk, piece // 2),
            vm(NZ, 2, 2, unit, piece // 2),
            vm(NZ, 2, unit, piece // 2),
            vm(NZ, 2, unit, piece // 2),
            vm(NZ, 2, unit, piece // 2),
            vm(NZ, 2, unit, piece // 2),
            vm(2, 2, tok, piece // 2),
            vm(2, tok, piece // 2),
            dma((10,)),
            dma,
            dma,
            dma((NZ,)),
            dma((NZ,)),
            dma((NZ,)),
            dma((NZ,)),
            dma((NZ, 2)),
            dma((NZ, 2)),
            dma((NZ, 2)),
            dma((NZ, 2)),
            dma((NZ, 2, 2)),
            dma((NZ, 2, 2)),
            dma((NZ, 2)),
            dma((NZ, 2)),
            dma((NZ, 2)),
            dma((NZ, 2)),
            dma((2,)),
            dma((2,)),
        ],
        compiler_params=pltpu.CompilerParams(
            collective_id=0, has_side_effects=True, vmem_limit_bytes=60 * 1024 * 1024
        ),
    )(
        tokens,
        route_ids.T,
        gate_weights.T,
        tenant_ids.reshape(1, tok),
        up_weight,
        down_weight,
        a_in_t,
        adapter_out,
    )


def per_device(
    tokens, route_ids, gate_weights, tenant_ids, up_weight, down_weight, adapter_in, adapter_out
):
    n_dp = lax.axis_size("dp")
    n_col = lax.axis_size("expert")
    tok_count = tokens.shape[0]
    chosen = route_ids.shape[1]
    features = tokens.shape[1]
    exp_local = up_weight.shape[0]
    piece = up_weight.shape[1]
    units = up_weight.shape[2]
    adapter_cols = adapter_in.shape[2]
    experts_all = exp_local * n_col
    capacity = max(2, 2 * tok_count * chosen // experts_all)
    send_rows = experts_all * capacity
    flat_routes = route_ids.reshape(-1)
    order = jnp.arange(flat_routes.shape[0], dtype=jnp.int32)
    same = flat_routes[:, None] == flat_routes[None, :]
    earlier = order[None, :] < order[:, None]
    rank = jnp.sum((same & earlier).astype(jnp.int32), axis=1)
    target = flat_routes * capacity + rank
    outgoing = (
        jnp.zeros((send_rows, features), jnp.bfloat16)
        .at[target]
        .set(jnp.repeat(tokens, chosen, axis=0))
    )
    tag_line = (
        jnp.full((send_rows,), -1.0, jnp.float32)
        .at[target]
        .set(jnp.repeat(tenant_ids, chosen).astype(jnp.float32))
    )
    tag_grid = jnp.broadcast_to(tag_line[:, None], (send_rows, n_dp)).astype(jnp.bfloat16)
    sending = outgoing.reshape(n_col, exp_local, capacity, n_dp, piece)
    tag_send = tag_grid.reshape(n_col, exp_local, capacity, n_dp, 1)
    arrived, arrived_tags = (
        lax.all_to_all(
            lax.all_to_all(sending, "dp", split_axis=3, concat_axis=2, tiled=True),
            "expert",
            split_axis=0,
            concat_axis=2,
            tiled=True,
        ),
        lax.all_to_all(
            lax.all_to_all(tag_send, "dp", split_axis=3, concat_axis=2, tiled=True),
            "expert",
            split_axis=0,
            concat_axis=2,
            tiled=True,
        ),
    )
    rows_all = arrived.shape[2]
    grid = arrived.reshape(exp_local, rows_all, piece)
    tags = arrived_tags.reshape(exp_local, rows_all).astype(jnp.float32)
    up_part = jnp.einsum("erd,edf->erf", grid, up_weight, preferred_element_type=jnp.float32)
    shrink_part = jnp.einsum("erd,edl->erl", grid, adapter_in, preferred_element_type=jnp.float32)
    owner = (jnp.arange(adapter_cols, dtype=jnp.int32) // RANK).astype(jnp.float32)
    shrink = lax.psum(shrink_part.astype(jnp.bfloat16), "dp").astype(jnp.float32)
    keep = owner[None, None, :] == tags[..., None]
    masked_values = jnp.where(keep, shrink, jnp.zeros((), jnp.float32))
    up_portion = lax.psum_scatter(
        up_part.astype(jnp.bfloat16), "dp", scatter_dimension=2, tiled=True
    ).astype(jnp.float32)
    share = units // n_dp
    mapping_portion = lax.dynamic_slice_in_dim(
        adapter_out, lax.axis_index("dp") * share, share, 2
    ).astype(jnp.float32)
    low_rank_adapter = jnp.einsum(
        "erl,elf->erf", masked_values, mapping_portion, precision=lax.Precision.HIGHEST
    )
    hidden_portion = jax.nn.silu(up_portion + low_rank_adapter).astype(jnp.bfloat16)
    hidden_activations = lax.all_gather(hidden_portion, "dp", axis=2, tiled=True)
    expert_out = jnp.einsum(
        "erf,efd->erd", hidden_activations, down_weight, preferred_element_type=jnp.float32
    ).astype(jnp.bfloat16)
    going_back = expert_out.reshape(1, exp_local, rows_all, 1, piece)
    returned = lax.all_to_all(
        lax.all_to_all(going_back, "expert", split_axis=2, concat_axis=0, tiled=True),
        "dp",
        split_axis=2,
        concat_axis=3,
        tiled=True,
    )
    results = returned.reshape(send_rows, features)
    picked = results[target].astype(jnp.float32).reshape(tok_count, chosen, features)
    mixed = jnp.sum(picked * gate_weights[:, :, None], axis=1)
    return mixed.astype(jnp.bfloat16)


def solution(mesh):
    placed = (
        P(("dp", "expert"), None),
        P(("dp", "expert"), None),
        P(("dp", "expert"), None),
        P(("dp", "expert")),
        P("expert", "dp", None),
        P("expert", None, "dp"),
        P("expert", "dp", None),
        P("expert", None, None),
    )
    small = mesh.shape["dp"] == 2 and mesh.shape["expert"] == 4 * NZ
    return jax.shard_map(
        fused if small else per_device, mesh=mesh, in_specs=placed, out_specs=P(("dp", "expert"), None), check_vma=False
    )
```
